32 devices in a mesh: grp: 4 (over y, core), seq: 8 (over z, x).
Axes of the slice: x: 2, y: 2, z: 4, core: 2. Of those that a mesh axis runs over, the one named last changes fastest.
Arguments:
- query: bfloat16 [4, 4096, 640], P('grp', 'seq'), may hold values from -64 to 64
- resp_kv: bfloat16 [4, 4096, 256], P('grp', 'seq'), may hold values from -6 to 6
- prompt_kv: bfloat16 [4, 2048, 256], P('grp', 'seq'), may hold values from -64 to 64
- grad_out: bfloat16 [4, 4096, 640], P('grp', 'seq'), may hold values from -6 to 6
- rewards: float32 [4, 16], P('grp'), may hold values from -4 to 4
- lengths: int32 [4, 16], P('grp'), may hold values from 1 to 256, as said below
- block_order: int32 [4, 32], P('grp'), may hold values from 0 to 31, each once within a row
Outputs:
- grad_query: bfloat16 [4, 4096, 640], P('grp', 'seq')
- grad_stream: bfloat16 [4, 4096, 256], P('grp', 'seq')
- grad_prompt: bfloat16 [4, 2048, 256], P('grp', 'seq')
The draws below stay inside these ranges and needn't reach their ends.
Inputs may be any that keep to these rules, and one draw needn't show every extreme that they name: `lengths`: each response has 1 to 256 tokens; some response has exactly 256. Each row of block_order names every response block of its group once.
All inputs are finite; a program needn't handle non-finite values.
Results may differ from the reference program's by a relative error of at most 0.015.
Values may be sent and summed in bfloat16 or wider, within the bound.
No kernel may reach another device: no remote copies, remote signals or barrier semaphores. Data moves between devices by JAX's collectives and lax.ppermute only.
A program may use at most 128 MiB of HBM per device.

```python
import jax
import jax.numpy as jnp
from jax import lax

HD = 128
QPK = 5
RESP = 16
BLK = 128
NB = 2
GROUPS = 4
PROMPT = 2048
NBLK = 32
STREAM = 4096


def draw_query(key, part):
    base_draw = jnp.clip(jax.random.normal(jax.random.fold_in(key, 1), (GROUPS, STREAM, QPK * HD), jnp.float32), -6.0, 6.0)
    return jnp.clip(base_draw, -64.0, 64.0).astype(jnp.bfloat16)


def draw_prompt_kv(key, part):
    base_draw = jnp.clip(jax.random.normal(jax.random.fold_in(key, 2), (GROUPS, PROMPT, 2 * HD), jnp.float32), -6.0, 6.0)
    return jnp.clip(base_draw, -64.0, 64.0).astype(jnp.bfloat16)


def draw_lengths(key, part):
    group_index = jnp.arange(GROUPS, dtype=jnp.int32)
    upper_len = jnp.maximum(NB * BLK * (GROUPS + 2 * group_index) // (3 * GROUPS - 2), 1)
    raw_bits = jax.random.randint(jax.random.fold_in(key, 5), (GROUPS, RESP), 0, 1 << 20, jnp.int32)
    half_span = (upper_len + 1) // 2
    drawn_lengths = upper_len[:, None] - raw_bits % half_span[:, None]
    full_slot = jax.random.randint(jax.random.fold_in(key, 6), (), 0, RESP, jnp.int32)
    drawn_lengths = drawn_lengths.at[GROUPS - 1, full_slot].set(NB * BLK)
    return drawn_lengths.astype(jnp.int32)


def block_scale(key, dims, cuts, least, top_value):
    def one(dim, blocks):
        heights = jax.random.uniform(jax.random.fold_in(jax.random.fold_in(key, 6), dim), (blocks,), jnp.float32, least / len(cuts), top_value / len(cuts))
        return jnp.repeat(jnp.exp(heights), dims[dim] // blocks).reshape((-1,) + (1,) * (len(dims) - dim - 1))

    level = one(*cuts[0])
    for cut in cuts[1:]:
        level = level * one(*cut)
    return level


def noise(rng, extent, scale, bound, cuts=(), kind=jnp.bfloat16):
    factor_of = block_scale(rng, extent, cuts, -0.22, 0.18) if cuts else 1.0
    values = jax.random.normal(rng, extent, jnp.float32) * scale * factor_of
    return jnp.minimum(jnp.maximum(values, -bound), bound).astype(kind)


def setup_inputs(seed: int = 0) -> dict:
    keys = jax.random.split(jax.random.key(seed), 8)
    return {
        "query": draw_query(jax.random.fold_in(keys[7], 71), 0),
        "resp_kv": noise(keys[1], (GROUPS, STREAM, 2 * HD), 1.0, 6.0, ((0, 4), (1, 8))),
        "prompt_kv": draw_prompt_kv(jax.random.fold_in(keys[7], 71), 0),
        "grad_out": noise(keys[3], (GROUPS, STREAM, QPK * HD), 1.0, 6.0, ((0, 4), (1, 8))),
        "rewards": noise(keys[4], (GROUPS, RESP), 1.0, 4.0, ((0, 4),), jnp.float32),
        "lengths": draw_lengths(jax.random.fold_in(keys[7], 71), 0),
        "block_order": jax.vmap(lambda own: jax.random.permutation(own, NBLK))(jax.random.split(keys[6], GROUPS)).reshape((GROUPS, NBLK)).astype(jnp.int32),
    }


LOSS_SCALE = 32.0
BIG_NEGATIVE = -1e30


def rounded(values):
    return lax.optimization_barrier(values.astype(jnp.bfloat16)).astype(jnp.float32)


def block_grads(query_block, weighted, prompt_pairs, own_pairs, positions):
    half_width = prompt_pairs.shape[1] // 2
    score_scale = half_width ** -0.5
    query_wide = query_block.astype(jnp.float32)
    prompt_keys = prompt_pairs[:, :half_width].astype(jnp.float32)
    prompt_values = prompt_pairs[:, half_width:].astype(jnp.float32)
    own_keys = own_pairs[:, :half_width].astype(jnp.float32)
    own_values = own_pairs[:, half_width:].astype(jnp.float32)
    visible = (jnp.arange(own_pairs.shape[0], dtype=jnp.int32)[None, :] <= positions[:, None])[None]
    scores_prompt = jnp.einsum("thd,kd->htk", query_wide, prompt_keys) * score_scale
    scores_own = jnp.where(visible, jnp.einsum("thd,kd->htk", query_wide, own_keys) * score_scale, BIG_NEGATIVE)
    peak_score = jnp.maximum(jnp.max(scores_prompt, axis=2), jnp.max(scores_own, axis=2))
    expo_prompt = jnp.exp(scores_prompt - peak_score[..., None])
    expo_own = jnp.where(visible, jnp.exp(scores_own - peak_score[..., None]), 0.0)
    prob_total = jnp.sum(expo_prompt, axis=2) + jnp.sum(expo_own, axis=2)
    probs_prompt = expo_prompt / prob_total[..., None]
    probs_own = expo_own / prob_total[..., None]
    low_prompt = rounded(probs_prompt)
    low_own = rounded(probs_own)
    attended = jnp.einsum("htk,kd->thd", low_prompt, prompt_values) + jnp.einsum("htk,kd->thd", low_own, own_values)
    row_delta = jnp.einsum("thd,thd->ht", weighted, attended)
    grad_prompt_scores = rounded(probs_prompt * (jnp.einsum("thd,kd->htk", weighted, prompt_values) - row_delta[..., None]))
    grad_own_scores = rounded(probs_own * (jnp.einsum("thd,kd->htk", weighted, own_values) - row_delta[..., None]))
    grad_query = (jnp.einsum("htk,kd->thd", grad_prompt_scores, prompt_keys) + jnp.einsum("htk,kd->thd", grad_own_scores, own_keys)) * score_scale
    prompt_term = jnp.concatenate([jnp.einsum("htk,thd->kd", grad_prompt_scores, query_wide) * score_scale, jnp.einsum("htk,thd->kd", low_prompt, weighted)], axis=1)
    own_term = jnp.concatenate([jnp.einsum("htk,thd->kd", grad_own_scores, query_wide) * score_scale, jnp.einsum("htk,thd->kd", low_own, weighted)], axis=1)
    return grad_query, prompt_term, own_term


def reference(query, resp_kv, prompt_kv, grad_out, rewards, lengths, block_order):
    count = jnp.sum(lengths).astype(jnp.float32)
    advantage = rewards - jnp.mean(rewards, axis=1, keepdims=True)
    factor = advantage * (LOSS_SCALE * GROUPS * RESP * NB * BLK) / count

    def one_group(group_inputs):
        group_query, group_pairs, group_prompt, group_grad, group_factor, group_lengths, block_plan = group_inputs
        inverse = jnp.argsort(block_plan).astype(jnp.int32)
        blocks = group_pairs.reshape(RESP * NB, BLK, 2 * HD)

        def block_step(carried, block_index):
            prompt_sum, stream_sum = carried
            stream_block = block_plan[block_index]
            response = stream_block // NB
            first_row = (stream_block % NB) * BLK
            slot_index = lax.dynamic_slice_in_dim(inverse, response * NB, NB)
            own_pairs = jnp.take(blocks, slot_index, axis=0).reshape(NB * BLK, 2 * HD)
            start_row = (block_index * BLK).astype(jnp.int32)
            query_block = lax.dynamic_slice_in_dim(group_query, start_row, BLK).reshape(BLK, QPK, HD)
            grad_block = lax.dynamic_slice_in_dim(group_grad, start_row, BLK)
            positions = first_row + jnp.arange(BLK, dtype=jnp.int32)
            token_weight = jnp.where(positions < group_lengths[response], group_factor[response], 0.0)
            weighted = rounded(grad_block.astype(jnp.float32) * token_weight[:, None]).reshape(BLK, QPK, HD)
            grad_query, prompt_term, own_term = block_grads(query_block, weighted, group_prompt, own_pairs, positions)
            stream_sum = stream_sum.at[slot_index].add(own_term.reshape(NB, BLK, 2 * HD))
            return (prompt_sum + prompt_term, stream_sum), grad_query.reshape(BLK, QPK * HD).astype(jnp.bfloat16)

        initial = (jnp.zeros((PROMPT, 2 * HD), jnp.float32), jnp.zeros((RESP * NB, BLK, 2 * HD), jnp.float32))
        (prompt_sum, stream_sum), grad_rows = lax.scan(block_step, initial, jnp.arange(RESP * NB, dtype=jnp.int32))
        return (grad_rows.reshape(STREAM, QPK * HD), stream_sum.reshape(STREAM, 2 * HD).astype(jnp.bfloat16), prompt_sum.astype(jnp.bfloat16))

    grad_query, grad_stream, grad_prompt = lax.map(one_group, (query, resp_kv, prompt_kv, grad_out, factor, lengths, block_order))
    return (grad_query, grad_stream, grad_prompt)
```

```python
from functools import partial

import jax
import jax.numpy as jnp
from jax import lax
from jax.experimental import pallas as pl
from jax.experimental.pallas import tpu as pltpu
from jax.sharding import PartitionSpec as P

RESP = 16
BLK = 128
NB = 2
LOSS_SCALE = 32.0
BIG_NEGATIVE = -1e30
LOG2E = 1.4426950408889634

F32 = jnp.float32
BF16 = jnp.bfloat16
NT = (((1,), (1,)), ((), ()))
TN = (((0,), (0,)), ((), ()))
NN = (((1,), (0,)), ((), ()))
TILE = 2 * BLK
VMEM = pl.BlockSpec(memory_space=pltpu.VMEM)
SMEM = pl.BlockSpec(memory_space=pltpu.SMEM)


def dot(a, b, dims):
    return lax.dot_general(a, b, dims, preferred_element_type=F32)


def call(kernel, name, out_shape, specs, args, scratch=(), flops=0, aliases=None):
    moved = sum(a.size * a.dtype.itemsize for a in args)
    return pl.pallas_call(
        kernel,
        name=name,
        out_shape=out_shape,
        in_specs=specs,
        out_specs=jax.tree.map(lambda _: VMEM, out_shape),
        scratch_shapes=list(scratch),
        input_output_aliases=aliases or {},
        compiler_params=pltpu.CompilerParams(vmem_limit_bytes=48 * 2**20),
        cost_estimate=pl.CostEstimate(flops=flops, bytes_accessed=moved, transcendentals=0),
    )(*args)


def split_kernel(count, kv_ref, *out_refs):
    me = lax.axis_index("seq")
    for k in range(count):
        for s in range(kv_ref.shape[0]):
            out_refs[k][s] = kv_ref[s, lax.bitwise_xor(me, k)]


def route_kernel(count, plan_ref, *refs):
    pieces, outs = refs[:count], refs[count : 2 * count]
    held, inverse = refs[2 * count :]
    me = lax.axis_index("seq")
    local = pieces[0].shape[0]
    for k in range(count):
        for s in range(local):
            held[lax.bitwise_xor(me, k) * local + s] = pieces[k][s]
    for j in range(plan_ref.shape[1]):
        inverse[plan_ref[0, j]] = j
    for k in range(count):
        for s in range(local):
            block = plan_ref[0, lax.bitwise_xor(me, k) * local + s]
            outs[k][s] = held[inverse[lax.bitwise_xor(block, 1)]]


def weight_kernel(groups, plan_ref, rewards_ref, grad_ref, *refs):
    lengths, out_ref = refs[:groups], refs[groups]
    me = lax.axis_index("seq")
    local = grad_ref.shape[0] // BLK
    total = jnp.int32(0)
    for ref in lengths:
        for r in range(RESP):
            total = total + ref[0, r]
    reward_sum = rewards_ref[0, 0]
    for r in range(1, RESP):
        reward_sum = reward_sum + rewards_ref[0, r]
    mean = reward_sum * (1.0 / RESP)
    count = jnp.full((BLK, 1), total.astype(F32))
    row = lax.broadcasted_iota(jnp.int32, (BLK, 1), 0)
    for s in range(local):
        block = plan_ref[0, me * local + s]
        response = lax.div(block, NB)
        first = lax.rem(block, NB) * BLK
        scaled = (rewards_ref[0, response] - mean) * (LOSS_SCALE * groups * RESP * NB * BLK)
        weight = jnp.where(row + first < lengths[0][0, response], scaled / count, 0.0)
        rows = slice(s * BLK, (s + 1) * BLK)
        out_ref[rows] = (grad_ref[rows].astype(F32) * weight).astype(BF16)


def head_tiles(q_ref):
    halves = q_ref.shape[0] // TILE
    return [
        (h * halves + r, r, slice(r * TILE, (r + 1) * TILE), slice(h * BLK, (h + 1) * BLK))
        for h in range(q_ref.shape[1] // BLK)
        for r in range(halves)
    ]


def by_block(pairs, side, rows, tile_rows):
    return jnp.concatenate(
        [
            dot(
                pairs[tile_rows * TILE + b * BLK : tile_rows * TILE + (b + 1) * BLK, side],
                rows[b * BLK : (b + 1) * BLK],
                NT,
            )
            for b in range(2)
        ],
        axis=1,
    )


KEYS = slice(0, BLK)
VALUES = slice(BLK, 2 * BLK)


def causal_mask():
    key = lax.broadcasted_iota(jnp.int32, (BLK, TILE), 0)
    row = lax.rem(lax.broadcasted_iota(jnp.int32, (BLK, TILE), 1), BLK)
    return key <= row


def odd_lanes(plan_ref, tile_rows, local):
    me = lax.axis_index("seq")
    lane = lax.broadcasted_iota(jnp.int32, (1, TILE), 1)
    odd = [lax.rem(plan_ref[0, me * local + 2 * tile_rows + b], NB) for b in range(2)]
    return jnp.where(lane < BLK, odd[0], odd[1]) > 0


def join_pieces(pieces, out_ref):
    count = len(pieces)
    me = lax.axis_index("seq")
    for k in range(count):
        for s in range(pieces[k].shape[0]):
            out_ref[s, lax.bitwise_xor(me, k)] = pieces[k][s]


def whole_blocks(held):
    local, count, rows, width = held.shape
    if rows % 16 == 0:
        return held[...].reshape(local * count * rows, width)
    return held[...].astype(F32).reshape(local * count * rows, width).astype(BF16)


def stats_kernel(scale, shards, own, parts, carried, *refs):
    refs = list(refs)
    plan_ref = refs.pop(0) if parts else None
    q_ref, w_ref = refs.pop(0), refs.pop(0)
    before = refs.pop(0) if carried else None
    kv = [refs.pop(0) for _ in range(shards)]
    own_ref = refs.pop(0) if own else None
    pieces = [refs.pop(0) for _ in range(parts)]
    out_ref = refs.pop(0)
    if parts:
        blocks_ref, held = refs
        join_pieces(pieces, held)
        blocks_ref[...] = whole_blocks(held)
    visible = causal_mask() if own else None
    for t, r, rows, cols in head_tiles(q_ref):
        q, w = q_ref[rows, cols], w_ref[rows, cols]
        if carried:
            m, l, d = before[t, 0:1], before[t, 1:2], before[t, 2:3]
        else:
            m = jnp.full((1, TILE), BIG_NEGATIVE, F32)
            l = d = jnp.zeros((1, TILE), F32)
        work = [(dot(ref[:, KEYS], q, NT), dot(ref[:, VALUES], w, NT)) for ref in kv]
        if own:
            s = by_block(own_ref, KEYS, q, r)
            work.append((jnp.where(visible, s, BIG_NEGATIVE), by_block(own_ref, VALUES, w, r)))
        if parts:
            s = by_block(blocks_ref, KEYS, q, r)
            seen = odd_lanes(plan_ref, r, q_ref.shape[0] // BLK)
            work.append((jnp.where(seen, s, BIG_NEGATIVE), by_block(blocks_ref, VALUES, w, r)))
        for s, dp in work:
            peak = jnp.maximum(m, jnp.max(s, axis=0, keepdims=True))
            shrink = jnp.exp2((m - peak) * scale)
            e = jnp.exp2(s * scale - peak * scale)
            l = l * shrink + jnp.sum(e, axis=0, keepdims=True)
            d = d * shrink + jnp.sum(e * dp, axis=0, keepdims=True)
            m = peak
        out_ref[t, 0:1] = m
        out_ref[t, 1:2] = l
        out_ref[t, 2:3] = d


def grad_kernel(scale, shards, inits, own, partner, carried, last, *refs):
    refs = list(refs)
    plan_ref = refs.pop(0) if partner else None
    q_ref, w_ref, stats_ref = refs.pop(0), refs.pop(0), refs.pop(0)
    before = refs.pop(0) if carried else None
    kv = [refs.pop(0) for _ in range(shards)]
    init = [[refs.pop(0) for _ in range(n)] for n in inits]
    own_ref = refs.pop(0) if own else None
    part_ref = refs.pop(0) if partner else None
    dq_ref = refs.pop(0)
    kv_out = [refs.pop(0) for _ in range(shards)]
    blocks_ref = own_ref if own else part_ref
    blocks_out = refs.pop(0) if own or partner else None
    kv_sum = refs.pop(0) if shards else None
    blocks_sum = refs.pop(0) if own or partner else None
    back = scale / LOG2E
    visible = causal_mask() if own else None
    per = kv[0].shape[0] if shards else 0
    if shards:
        keys = jnp.concatenate([ref[:, KEYS] for ref in kv], axis=0)
        values = jnp.concatenate([ref[:, VALUES] for ref in kv], axis=0)
    for t, r, rows, cols in head_tiles(q_ref):
        q, w = q_ref[rows, cols], w_ref[rows, cols]
        peak = stats_ref[t, 0:1] * scale
        inverse = 1.0 / stats_ref[t, 1:2]
        delta = stats_ref[t, 2:3] * inverse

        def grads(s, dp):
            p = jnp.exp2(s * scale - peak) * inverse
            return p.astype(BF16), (p * (dp - delta)).astype(BF16)

        dq = None
        if shards:
            p, ds = grads(dot(keys, q, NT), dot(values, w, NT))
            dk, dv = dot(ds, q, NN), dot(p, w, NN)
            if t == 0:
                kv_sum[:, KEYS] = dk
                kv_sum[:, VALUES] = dv
            else:
                kv_sum[:, KEYS] += dk
                kv_sum[:, VALUES] += dv
            dq = dot(ds, keys, TN)
        if own or partner:
            s = by_block(blocks_ref, KEYS, q, r)
            seen = visible if own else odd_lanes(plan_ref, r, q_ref.shape[0] // BLK)
            s = jnp.where(seen, s, BIG_NEGATIVE)
            p, ds = grads(s, by_block(blocks_ref, VALUES, w, r))
            turned = []
            for b in range(2):
                lanes = slice(b * BLK, (b + 1) * BLK)
                place = slice(r * TILE + b * BLK, r * TILE + (b + 1) * BLK)
                dk, dv = dot(ds[:, lanes], q[lanes], NN), dot(p[:, lanes], w[lanes], NN)
                if cols.start == 0:
                    blocks_sum[place, KEYS] = dk
                    blocks_sum[place, VALUES] = dv
                else:
                    blocks_sum[place, KEYS] += dk
                    blocks_sum[place, VALUES] += dv
                turned.append(dot(ds[:, lanes], blocks_ref[place, KEYS], TN))
            turned = jnp.concatenate(turned, axis=0)
            dq = turned if dq is None else dq + turned
        if carried:
            dq = dq + before[rows, cols]
        dq_ref[rows, cols] = (dq * back).astype(BF16) if last else dq
    for i in range(shards):
        place = slice(i * per, (i + 1) * per)
        for side, factor in ((KEYS, back), (VALUES, 1.0)):
            total = kv_sum[place, side] * factor
            for ref in init[i]:
                total = total + ref[:, side].astype(F32)
            kv_out[i][:, side] = total.astype(kv_out[i].dtype)
    if own or partner:
        for side, factor in ((KEYS, back), (VALUES, 1.0)):
            total = blocks_sum[:, side] * factor
            blocks_out[:, side] = total.astype(blocks_out.dtype)


def finish_kernel(count, plan_ref, own_ref, *refs):
    pieces, out_ref, held = refs[:count], refs[count], refs[count + 1]
    me = lax.axis_index("seq")
    local = own_ref.shape[0] // BLK
    join_pieces(pieces, held)
    joined = whole_blocks(held)
    for s in range(local):
        rows = slice(s * BLK, (s + 1) * BLK)
        odd = lax.rem(plan_ref[0, me * local + s], NB)
        odd_rows = jnp.full((BLK, 2 * BLK), odd, jnp.int32) > 0
        extra = jnp.where(odd_rows, 0.0, joined[rows].astype(F32))
        out_ref[rows] = (own_ref[rows] + extra).astype(BF16)


def total_kernel(*refs):
    total = refs[0][...]
    for ref in refs[1:-1]:
        total = total + ref[...].astype(F32)
    refs[-1][...] = total.astype(BF16)


def local(query, resp_kv, prompt_kv, grad_out, rewards, lengths, block_order):
    groups = lax.axis_size("grp")
    count = lax.axis_size("seq")
    q, resp, prompt, grad = query[0], resp_kv[0], prompt_kv[0], grad_out[0]
    rows, width = resp.shape
    blocks = rows // BLK
    heads = q.shape[1] // BLK
    scale = LOG2E * BLK**-0.5
    piece = jax.ShapeDtypeStruct((blocks, BLK // count, width), BF16)
    apart = pltpu.VMEM((blocks, count, BLK // count, width), BF16)

    def swap(x, axis, k):
        size = lax.axis_size(axis)
        return lax.ppermute(x, axis, [(i, i ^ k) for i in range(size)])

    def exchange(sent):
        return [sent[0]] + [swap(sent[k], "seq", k) for k in range(1, count)]

    def route(name, arrived):
        return call(
            partial(route_kernel, count),
            name,
            [piece] * count,
            [SMEM] + [VMEM] * count,
            [block_order, *arrived],
            [
                pltpu.VMEM((blocks * count, BLK // count, width), BF16),
                pltpu.SMEM((block_order.shape[1],), jnp.int32),
            ],
        )

    def split(name, x):
        return call(
            partial(split_kernel, count),
            name,
            [piece] * count,
            [VMEM],
            [x.reshape(blocks, count, BLK // count, width)],
        )

    lengths_all = [lengths] + [swap(lengths, "grp", k) for k in range(1, groups)]
    pieces = exchange(split("split_pairs", resp))
    column = {0: prompt}
    for k in range(2, count, 2):
        column[k] = swap(prompt, "seq", k)
    across = {k: swap(column[k], "seq", 1) for k in column}
    weighted = call(
        partial(weight_kernel, groups),
        "weight_rows",
        jax.ShapeDtypeStruct(grad.shape, BF16),
        [SMEM, SMEM, VMEM] + [SMEM] * groups,
        [block_order, rewards, grad, *lengths_all],
    )
    arrived = exchange(route("route_pairs", pieces))

    stats_shape = jax.ShapeDtypeStruct((heads * rows // TILE, 8, TILE), F32)
    product_flops = 2 * rows * heads * BLK

    def stats(name, before, kv, own=None, parts=()):
        args, specs = [], []
        if parts:
            args, specs = [block_order], [SMEM]
        args += [q, weighted]
        args += [before] if before is not None else []
        args += list(kv) + ([own] if own is not None else []) + list(parts)
        specs += [VMEM] * (len(args) - len(specs))
        keys = sum(x.shape[0] for x in kv) + BLK * ((own is not None) + bool(parts))
        out = stats_shape
        scratch = []
        if parts:
            out = [stats_shape, jax.ShapeDtypeStruct(resp.shape, BF16)]
            scratch = [apart]
        return call(
            partial(stats_kernel, scale, len(kv), own is not None, len(parts), before is not None),
            name,
            out,
            specs,
            args,
            scratch,
            flops=2 * keys * product_flops,
        )

    state = stats("stats_own", None, [prompt], own=resp)
    for k in range(2, count, 2):
        state = stats("stats_prompt", state, [across[k - 2], column[k]])
    state, partner = stats("stats_last", state, [across[count - 2]], parts=arrived)

    def grads(name, before, kv, init=None, own=None, part=None, last=False, kinds=None):
        init = init or [[] for _ in kv]
        args, specs = ([block_order], [SMEM]) if part is not None else ([], [])
        args += [q, weighted, state]
        args += [before] if before is not None else []
        args += list(kv) + [x for xs in init for x in xs]
        args += [own] if own is not None else []
        args += [part] if part is not None else []
        specs += [VMEM] * (len(args) - len(specs))
        out = [jax.ShapeDtypeStruct(q.shape, BF16 if last else F32)]
        out += [jax.ShapeDtypeStruct(x.shape, d) for x, d in zip(kv, kinds or [BF16] * len(kv))]
        scratch = []
        keys = sum(x.shape[0] for x in kv)
        if kv:
            scratch.append(pltpu.VMEM((keys, width), F32))
        if own is not None or part is not None:
            out.append(jax.ShapeDtypeStruct(resp.shape, F32 if own is not None else BF16))
            scratch.append(pltpu.VMEM(resp.shape, F32))
            keys += BLK
        return call(
            partial(
                grad_kernel,
                scale,
                len(kv),
                tuple(len(xs) for xs in init),
                own is not None,
                part is not None,
                before is not None,
                last,
            ),
            name,
            out,
            specs,
            args,
            scratch,
            flops=5 * keys * product_flops,
        )

    dq, partner_terms = grads("grads_partner", None, [], part=partner)
    backward = exchange(split("split_terms", partner_terms))
    even = list(range(0, count, 2))
    dq, *far = grads("grads_across", dq, [across[k] for k in even])
    far = {k: swap(x, "seq", 1) for k, x in zip(even, far)}
    dq, *mid = grads(
        "grads_column", dq, [column[k] for k in even[1:]], init=[[far[k]] for k in even[1:]]
    )
    mid = [swap(x, "seq", k) for k, x in zip(even[1:], mid)]
    returned = exchange(route("route_terms", backward))
    dq, near, own_terms = grads(
        "grads_own", dq, [prompt], init=[[far[0]]], own=resp, last=True, kinds=[F32]
    )
    grad_prompt = call(
        total_kernel,
        "sum_prompt",
        jax.ShapeDtypeStruct(prompt.shape, BF16),
        [VMEM] * (1 + len(mid)),
        [near, *mid],
    )
    grad_stream = call(
        partial(finish_kernel, count),
        "sum_stream",
        jax.ShapeDtypeStruct(resp.shape, BF16),
        [SMEM, VMEM] + [VMEM] * count,
        [block_order, own_terms, *returned],
        [apart],
    )
    return dq[None], grad_stream[None], grad_prompt[None]


def solution(mesh):
    in_specs = (
        P("grp", "seq", None),
        P("grp", "seq", None),
        P("grp", "seq", None),
        P("grp", "seq", None),
        P("grp", None),
        P("grp", None),
        P("grp", None),
    )
    out_specs = (P("grp", "seq", None), P("grp", "seq", None), P("grp", "seq", None))
    return jax.shard_map(local, mesh=mesh, in_specs=in_specs, out_specs=out_specs, check_vma=False)
```

```python
from functools import partial

import jax
import jax.numpy as jnp
from jax import lax
from jax.experimental import pallas as pl
from jax.experimental.pallas import tpu as pltpu
from jax.sharding import PartitionSpec as P

RESP = 16
BLK = 128
NB = 2
LOSS_SCALE = 32.0
BIG_NEGATIVE = -1e30
LOG2E = 1.4426950408889634

F32 = jnp.float32
BF16 = jnp.bfloat16
NT = (((1,), (1,)), ((), ()))
TN = (((0,), (0,)), ((), ()))
NN = (((1,), (0,)), ((), ()))
TILE = 2 * BLK
VMEM = pl.BlockSpec(memory_space=pltpu.VMEM)
SMEM = pl.BlockSpec(memory_space=pltpu.SMEM)


def dot(a, b, dims):
    return lax.dot_general(a, b, dims, preferred_element_type=F32)


def call(kernel, name, out_shape, specs, args, scratch=(), flops=0, aliases=None):
    moved = sum(a.size * a.dtype.itemsize for a in args)
    return pl.pallas_call(
        kernel,
        name=name,
        out_shape=out_shape,
        in_specs=specs,
        out_specs=jax.tree.map(lambda _: VMEM, out_shape),
        scratch_shapes=list(scratch),
        input_output_aliases=aliases or {},
        compiler_params=pltpu.CompilerParams(vmem_limit_bytes=24 * 2**20),
        cost_estimate=pl.CostEstimate(flops=4 * flops, bytes_accessed=moved, transcendentals=0),
    )(*args)


def write_pieces(pairs_ref, out_refs):
    line = lax.div(lax.axis_index("seq"), 2)
    rows = BLK // len(out_refs)
    for k, out_ref in enumerate(out_refs):
        first = lax.bitwise_xor(line, k) * rows
        for s in range(out_ref.shape[0]):
            place = pl.ds(pl.multiple_of(s * BLK + first, rows), rows)
            out_ref[s] = pairs_ref[place].astype(BF16)


def split_kernel(kv_ref, *out_refs):
    write_pieces(kv_ref, out_refs)


def stack_kernel(*refs):
    for k, ref in enumerate(refs[:-1]):
        refs[-1][k] = ref[...]


def route_kernel(plan_ref, mine_ref, other_ref, *refs):
    outs, held, inverse = refs[:-2], refs[-2], refs[-1]
    me = lax.axis_index("seq")
    line, side = lax.div(me, 2), lax.rem(me, 2)
    held[side] = mine_ref[...]
    held[1 - side] = other_ref[...]
    local = mine_ref.shape[1]
    for j in range(plan_ref.shape[1]):
        inverse[plan_ref[0, j]] = j
    for k, out_ref in enumerate(outs):
        device = lax.bitwise_xor(line, k) * 2 + side
        for s in range(local):
            partner = inverse[lax.bitwise_xor(plan_ref[0, device * local + s], 1)]
            owner = lax.div(partner, local)
            place = lax.bitwise_xor(lax.div(owner, 2), line)
            out_ref[s] = held[lax.rem(owner, 2), place, lax.rem(partner, local)]


def join_pieces(pieces, out_ref):
    line = lax.div(lax.axis_index("seq"), 2)
    rows = BLK // len(pieces)
    for k, ref in enumerate(pieces):
        first = lax.bitwise_xor(line, k) * rows
        for s in range(ref.shape[0]):
            out_ref[pl.ds(pl.multiple_of(s * BLK + first, rows), rows)] = ref[s]


def weight_kernel(groups, plan_ref, rewards_ref, grad_ref, *refs):
    lengths, out_ref = refs[:groups], refs[groups]
    me = lax.axis_index("seq")
    local = grad_ref.shape[0] // BLK
    total = jnp.int32(0)
    for ref in lengths:
        for r in range(RESP):
            total = total + ref[0, r]
    reward_sum = rewards_ref[0, 0]
    for r in range(1, RESP):
        reward_sum = reward_sum + rewards_ref[0, r]
    mean = reward_sum * (1.0 / RESP)
    count = jnp.full((BLK, 1), total.astype(F32))
    row = lax.broadcasted_iota(jnp.int32, (BLK, 1), 0)
    for s in range(local):
        block = plan_ref[0, me * local + s]
        response = lax.div(block, NB)
        first = lax.rem(block, NB) * BLK
        scaled = (rewards_ref[0, response] - mean) * (LOSS_SCALE * groups * RESP * NB * BLK)
        weight = jnp.where(row + first < lengths[0][0, response], scaled / count, 0.0)
        rows = slice(s * BLK, (s + 1) * BLK)
        out_ref[rows] = (grad_ref[rows].astype(F32) * weight).astype(BF16)


def head_tiles(q_ref):
    halves = q_ref.shape[0] // TILE
    return [
        (h * halves + r, r, slice(r * TILE, (r + 1) * TILE), slice(h * BLK, (h + 1) * BLK))
        for h in range(q_ref.shape[1] // BLK)
        for r in range(halves)
    ]


KEYS = slice(0, BLK)
VALUES = slice(BLK, 2 * BLK)


def block_rows(ref, j):
    rows = slice(j * BLK, (j + 1) * BLK)
    heads = ref.shape[1] // BLK
    return jnp.concatenate([ref[rows, h * BLK : (h + 1) * BLK] for h in range(heads)], axis=0)


def block_seen(plan_ref, j, local, heads):
    if plan_ref is None:
        key = lax.broadcasted_iota(jnp.int32, (BLK, BLK), 0)
        row = lax.broadcasted_iota(jnp.int32, (BLK, BLK), 1)
        return jnp.concatenate([key <= row] * heads, axis=1)
    me = lax.axis_index("seq")
    odd = lax.rem(plan_ref[0, me * local + j], NB)
    return jnp.full((BLK, heads * BLK), odd, jnp.int32) > 0


def merged(scale, first, second):
    peak = jnp.maximum(first[0], second[0])
    a, b = jnp.exp2((first[0] - peak) * scale), jnp.exp2((second[0] - peak) * scale)
    return peak, first[1] * a + second[1] * b, first[2] * a + second[2] * b


def score_stats(scale, s, dp):
    peak = jnp.max(s, axis=0, keepdims=True)
    e = jnp.exp2(s * scale - peak * scale)
    return peak, jnp.sum(e, axis=0, keepdims=True), jnp.sum(e * dp, axis=0, keepdims=True)


def stats_kernel(scale, shards, own, parts, carried, *refs):
    refs = list(refs)
    plan_ref = refs.pop(0) if parts else None
    q_ref, w_ref = refs.pop(0), refs.pop(0)
    before = refs.pop(0) if carried else None
    kv = [refs.pop(0) for _ in range(shards)]
    own_ref = refs.pop(0) if own else None
    pieces = [refs.pop(0) for _ in range(parts)]
    out_ref = refs.pop(0)
    heads, local = q_ref.shape[1] // BLK, q_ref.shape[0] // BLK
    block_stats = None
    if parts:
        own_ref = refs.pop(0)
        join_pieces(pieces, own_ref)
    if own_ref is not None:
        block_stats = []
        for j in range(local):
            pairs = own_ref[j * BLK : (j + 1) * BLK]
            s = dot(pairs[:, KEYS], block_rows(q_ref, j), NT)
            dp = dot(pairs[:, VALUES], block_rows(w_ref, j), NT)
            s = jnp.where(block_seen(plan_ref, j, local, heads), s, BIG_NEGATIVE)
            block_stats.append(score_stats(scale, s, dp))
    for t, r, rows, cols in head_tiles(q_ref):
        q, w = q_ref[rows, cols], w_ref[rows, cols]
        state = None
        if carried:
            state = tuple(before[t, i : i + 1] for i in range(3))
        if block_stats is not None:
            pair = block_stats[2 * r : 2 * r + 2]
            more = tuple(jnp.concatenate([x[i][:, cols] for x in pair], axis=1) for i in range(3))
            state = more if state is None else merged(scale, state, more)
        for ref in kv:
            s, dp = dot(ref[:, KEYS], q, NT), dot(ref[:, VALUES], w, NT)
            if state is None:
                state = score_stats(scale, s, dp)
                continue
            m, l, d = state
            peak = jnp.maximum(m, jnp.max(s, axis=0, keepdims=True))
            shrink = jnp.exp2((m - peak) * scale)
            e = jnp.exp2(s * scale - peak * scale)
            l = l * shrink + jnp.sum(e, axis=0, keepdims=True)
            d = d * shrink + jnp.sum(e * dp, axis=0, keepdims=True)
            state = peak, l, d
        for i in range(3):
            out_ref[t, i : i + 1] = state[i]


def grad_kernel(scale, shards, inits, own, partner, carried, last, *refs):
    refs = list(refs)
    plan_ref = refs.pop(0) if partner else None
    q_ref, w_ref, stats_ref = refs.pop(0), refs.pop(0), refs.pop(0)
    before = refs.pop(0) if carried else None
    kv = [refs.pop(0) for _ in range(shards)]
    init = [refs.pop(0) for _ in range(inits)]
    blocks_ref = refs.pop(0) if own or partner else None
    dq_ref = refs.pop(0)
    kv_out = refs.pop(0) if shards else None
    blocks_out = refs if partner else refs.pop(0) if own else None
    if partner:
        blocks_out, blocks_sum = refs[:partner], refs[partner]
    elif own:
        blocks_sum = blocks_out
    kv_sum, dq_part = (refs[0], refs[1]) if shards and own else (refs[0] if shards else None, dq_ref)
    heads, local = q_ref.shape[1] // BLK, q_ref.shape[0] // BLK
    halves = q_ref.shape[0] // TILE
    back = scale / LOG2E

    def factors(rows):
        inverse = 1.0 / rows[1]
        return rows[0] * scale, inverse, rows[2] * inverse

    def grads(s, dp, rows):
        peak, inverse, delta = rows
        p = jnp.exp2(s * scale - peak) * inverse
        return p.astype(BF16), (p * (dp - delta)).astype(BF16)

    if blocks_ref is not None:
        for j in range(local):
            place = slice(j * BLK, (j + 1) * BLK)
            lanes = slice((j % 2) * BLK, (j % 2 + 1) * BLK)
            rows = [
                jnp.concatenate(
                    [stats_ref[h * halves + j // 2, i : i + 1, lanes] for h in range(heads)], axis=1
                )
                for i in range(3)
            ]
            q, w = block_rows(q_ref, j), block_rows(w_ref, j)
            keys = blocks_ref[place, KEYS]
            s = jnp.where(block_seen(plan_ref, j, local, heads), dot(keys, q, NT), BIG_NEGATIVE)
            p, ds = grads(s, dot(blocks_ref[place, VALUES], w, NT), factors(rows))
            blocks_sum[place, KEYS] = dot(ds, q, NN) * back
            blocks_sum[place, VALUES] = dot(p, w, NN)
            dq = dot(ds, keys, TN)
            for h in range(heads):
                dq_part[place, h * BLK : (h + 1) * BLK] = dq[h * BLK : (h + 1) * BLK]
        if partner:
            write_pieces(blocks_sum, blocks_out)
    if not shards:
        return
    per = kv[0].shape[0]
    keys = jnp.concatenate([ref[:, KEYS] for ref in kv], axis=0)
    values = jnp.concatenate([ref[:, VALUES] for ref in kv], axis=0)
    for t, r, rows, cols in head_tiles(q_ref):
        q, w = q_ref[rows, cols], w_ref[rows, cols]
        state = factors([stats_ref[t, i : i + 1] for i in range(3)])
        p, ds = grads(dot(keys, q, NT), dot(values, w, NT), state)
        dk, dv = dot(ds, q, NN), dot(p, w, NN)
        if t == 0:
            kv_sum[:, KEYS] = dk
            kv_sum[:, VALUES] = dv
        else:
            kv_sum[:, KEYS] += dk
            kv_sum[:, VALUES] += dv
        dq = dot(ds, keys, TN)
        if own:
            dq = dq + dq_part[rows, cols]
        if carried:
            dq = dq + before[rows, cols]
        dq_ref[rows, cols] = (dq * back).astype(BF16) if last else dq
    for side, factor in ((KEYS, back), (VALUES, 1.0)):
        total = kv_sum[:, side] * factor
        for ref in init:
            total = total + ref[:, side].astype(F32)
        kv_out[:, side] = total.astype(kv_out.dtype)


def finish_kernel(plan_ref, own_ref, *refs):
    pieces, out_ref, held = refs[:-2], refs[-2], refs[-1]
    me = lax.axis_index("seq")
    local = own_ref.shape[0] // BLK
    join_pieces(pieces, held)
    for s in range(local):
        rows = slice(s * BLK, (s + 1) * BLK)
        odd = lax.rem(plan_ref[0, me * local + s], NB)
        odd_rows = jnp.full((BLK, 2 * BLK), odd, jnp.int32) > 0
        extra = jnp.where(odd_rows, 0.0, held[rows].astype(F32))
        out_ref[rows] = (own_ref[rows] + extra).astype(BF16)


def pick_kernel(per, parts, picked, *refs):
    out_ref = refs[-1]
    where = []
    for ref in refs[:parts]:
        where += [(ref, i) for i in range(ref.shape[0] // per)]
    for n, i in enumerate(picked):
        ref, at = where[i]
        total = ref[at * per : (at + 1) * per].astype(F32)
        for other in refs[parts:-1]:
            total = total + other[i * per : (i + 1) * per].astype(F32)
        out_ref[n * per : (n + 1) * per] = total.astype(out_ref.dtype)


def local(query, resp_kv, prompt_kv, grad_out, rewards, lengths, block_order):
    groups = lax.axis_size("grp")
    count = lax.axis_size("seq")
    q, resp, prompt, grad = query[0], resp_kv[0], prompt_kv[0], grad_out[0]
    rows, width = resp.shape
    blocks = rows // BLK
    heads = q.shape[1] // BLK
    line = count // 2
    scale = LOG2E * BLK**-0.5
    piece = jax.ShapeDtypeStruct((blocks, BLK // line, width), BF16)
    stack = jax.ShapeDtypeStruct((line, *piece.shape), BF16)

    def swap(x, axis, k):
        size = lax.axis_size(axis)
        return lax.ppermute(x, axis, [(i, i ^ k) for i in range(size)])

    def along(sent):
        return [sent[0]] + [swap(sent[k], "seq", 2 * k) for k in range(1, line)]

    def route(name, sent):
        mine = call(stack_kernel, name + "_stack", stack, [VMEM] * line, along(sent))
        other = swap(mine, "seq", 1)
        routed = call(
            route_kernel,
            name + "_route",
            [piece] * line,
            [SMEM, VMEM, VMEM],
            [block_order, mine, other],
            [pltpu.VMEM((2, *stack.shape), BF16), pltpu.SMEM((block_order.shape[1],), jnp.int32)],
        )
        return along(routed)

    lengths_all = [lengths] + [swap(lengths, "grp", k) for k in range(1, groups)]
    arrived = route("pairs", call(split_kernel, "pairs_split", [piece] * line, [VMEM], [resp]))
    column = {0: prompt}
    bit = count // 2
    while bit > 1:
        column.update({k ^ bit: swap(x, "seq", bit) for k, x in column.items()})
        bit //= 2
    across = {k: swap(x, "seq", 1) for k, x in column.items()}
    weighted = call(
        partial(weight_kernel, groups),
        "weight_rows",
        jax.ShapeDtypeStruct(grad.shape, BF16),
        [SMEM, SMEM, VMEM] + [SMEM] * groups,
        [block_order, rewards, grad, *lengths_all],
    )

    stats_shape = jax.ShapeDtypeStruct((heads * rows // TILE, 8, TILE), F32)
    product_flops = 2 * rows * heads * BLK

    def stats(name, before, kv, own=None, parts=()):
        args = [block_order] if parts else []
        specs = [SMEM] * len(args)
        args += [q, weighted] + ([before] if before is not None else []) + list(kv)
        args += ([own] if own is not None else []) + list(parts)
        specs += [VMEM] * (len(args) - len(specs))
        keys = sum(x.shape[0] for x in kv) + BLK * ((own is not None) + bool(parts))
        return call(
            partial(stats_kernel, scale, len(kv), own is not None, len(parts), before is not None),
            name,
            [stats_shape, jax.ShapeDtypeStruct(resp.shape, BF16)] if parts else stats_shape,
            specs,
            args,
            flops=2 * keys * product_flops,
        )

    state = stats("stats_own", None, [prompt], own=resp)
    coming = [x for k, x in column.items() if k] + list(across.values())
    while len(coming) > 1:
        state = stats("stats_prompt", state, coming[:2])
        coming = coming[2:]
    state, partner = stats("stats_last", state, coming, parts=arrived)

    def grads(name, before, kv, init=(), own=None, part=None, last=False, kind=BF16):
        args = [block_order] if part is not None else []
        specs = [SMEM] * len(args)
        args += [q, weighted, state] + ([before] if before is not None else [])
        args += list(kv) + list(init) + [x for x in (own, part) if x is not None]
        specs += [VMEM] * (len(args) - len(specs))
        keys = sum(x.shape[0] for x in kv)
        out = [jax.ShapeDtypeStruct(q.shape, BF16 if last else F32)]
        out += [jax.ShapeDtypeStruct((keys, width), kind)] if kv else []
        scratch = [pltpu.VMEM((keys, width), F32)] if kv else []
        if own is not None:
            out.append(jax.ShapeDtypeStruct(resp.shape, F32))
            scratch.append(pltpu.VMEM(q.shape, F32))
        if part is not None:
            out += [piece] * line
            scratch.append(pltpu.VMEM(resp.shape, F32))
        body = partial(
            grad_kernel,
            scale,
            len(kv),
            len(init),
            own is not None,
            line if part is not None else 0,
            before is not None,
            last,
        )
        flops = 5 * (keys + BLK * ((own is not None) + (part is not None))) * product_flops
        return call(body, name, out, specs, args, scratch, flops=flops)

    per = prompt.shape[0]
    near = [k for k in column if k & 2]
    rest = [k for k in column if not k & 2]
    dq, *terms = grads("grads_partner", None, [], part=partner)
    returned = route("terms", terms)
    dq, far_near = grads("grads_across", dq, [across[k] for k in near])
    far_near = swap(far_near, "seq", 1)
    dq, far_rest = grads("grads_across", dq, [across[k] for k in rest])
    far_rest = swap(far_rest, "seq", 1)
    dq, sums = grads("grads_near", dq, [column[k] for k in near], init=[far_near])
    sums = swap(sums, "seq", 2)
    held = rest
    dq, mine, own_terms = grads("grads_own", dq, [column[k] for k in rest[:1]], own=resp, kind=F32)
    dq, others = grads("grads_rest", dq, [column[k] for k in rest[1:]], last=True, kind=F32)
    parts = [mine, others]
    extra = [far_rest, sums]
    raise_to = 4
    grad_prompt = None
    while raise_to < count:
        keep = [i for i, k in enumerate(held) if not k & raise_to]
        send = [i for i, k in enumerate(held) if k & raise_to]
        sent = call(
            partial(pick_kernel, per, len(parts), tuple(send)),
            "sum_far",
            jax.ShapeDtypeStruct((per * len(send), width), BF16),
            [VMEM] * (len(parts) + len(extra)),
            [*parts, *extra],
        )
        received = swap(sent, "seq", raise_to)
        kept = call(
            partial(pick_kernel, per, len(parts), tuple(keep)),
            "sum_near",
            jax.ShapeDtypeStruct((per * len(keep), width), F32),
            [VMEM] * (len(parts) + len(extra)),
            [*parts, *extra],
        )
        held, parts, extra = [held[i] for i in keep], [kept], [received]
        raise_to *= 2
    grad_prompt = call(
        partial(pick_kernel, per, len(parts), (0,)),
        "sum_prompt",
        jax.ShapeDtypeStruct(prompt.shape, BF16),
        [VMEM] * (len(parts) + len(extra)),
        [*parts, *extra],
    )
    grad_stream = call(
        finish_kernel,
        "sum_stream",
        jax.ShapeDtypeStruct(resp.shape, BF16),
        [SMEM, VMEM] + [VMEM] * line,
        [block_order, own_terms, *returned],
        [pltpu.VMEM(resp.shape, BF16)],
    )
    return dq[None], grad_stream[None], grad_prompt[None]


def solution(mesh):
    in_specs = (
        P("grp", "seq", None),
        P("grp", "seq", None),
        P("grp", "seq", None),
        P("grp", "seq", None),
        P("grp", None),
        P("grp", None),
        P("grp", None),
    )
    out_specs = (P("grp", "seq", None), P("grp", "seq", None), P("grp", "seq", None))
    return jax.shard_map(local, mesh=mesh, in_specs=in_specs, out_specs=out_specs, check_vma=False)
```

```python
from functools import partial

import jax
import jax.numpy as jnp
from jax import lax
from jax.experimental import pallas as pl
from jax.experimental.pallas import tpu as pltpu
from jax.sharding import PartitionSpec as P

RESP = 16
BLK = 128
NB = 2
LOSS_SCALE = 32.0
BIG_NEGATIVE = -1e30
COVER = 7 * 10**9
LOG2E = 1.4426950408889634

F32 = jnp.float32
BF16 = jnp.bfloat16
NT = (((1,), (1,)), ((), ()))
TN = (((0,), (0,)), ((), ()))
NN = (((1,), (0,)), ((), ()))
TILE = 2 * BLK
VMEM = pl.BlockSpec(memory_space=pltpu.VMEM)
SMEM = pl.BlockSpec(memory_space=pltpu.SMEM)
ANY = pl.BlockSpec(memory_space=pl.ANY)


def dot(a, b, dims):
    return lax.dot_general(a, b, dims, preferred_element_type=F32)


def call(kernel, name, out_shape, specs, args, scratch=(), after=(), beside=False):
    specs, args = [*specs, *[ANY] * len(after)], [*args, *after]
    return pl.pallas_call(
        kernel,
        name=name,
        out_shape=out_shape,
        in_specs=specs,
        out_specs=jax.tree.map(lambda _: VMEM, out_shape),
        scratch_shapes=list(scratch),
        compiler_params=pltpu.CompilerParams(vmem_limit_bytes=24 * 2**20),
        cost_estimate=pl.CostEstimate(flops=COVER * beside, bytes_accessed=0, transcendentals=0),
    )(*args)


def write_pieces(pairs_ref, out_refs):
    line = lax.div(lax.axis_index("seq"), 2)
    rows = BLK // len(out_refs)
    for k, out_ref in enumerate(out_refs):
        first = lax.bitwise_xor(line, k) * rows
        for s in range(out_ref.shape[0]):
            place = pl.ds(pl.multiple_of(s * BLK + first, rows), rows)
            out_ref[s] = pairs_ref[place].astype(BF16)


def split_kernel(kv_ref, *out_refs):
    write_pieces(kv_ref, out_refs)


def stack_kernel(count, *refs):
    for k in range(count):
        refs[-1][k] = refs[k][...]


def pass_kernel(x_ref, after_ref, out_ref):
    out_ref[...] = x_ref[...]


def route_kernel(count, plan_ref, mine_ref, other_ref, *refs):
    outs, held, inverse = refs[len(refs) - 2 - count : -2], refs[-2], refs[-1]
    me = lax.axis_index("seq")
    line, side = lax.div(me, 2), lax.rem(me, 2)
    held[side] = mine_ref[...]
    held[1 - side] = other_ref[...]
    local = mine_ref.shape[1]
    for j in range(plan_ref.shape[1]):
        inverse[plan_ref[0, j]] = j
    for k, out_ref in enumerate(outs):
        device = lax.bitwise_xor(line, k) * 2 + side
        for s in range(local):
            partner = inverse[lax.bitwise_xor(plan_ref[0, device * local + s], 1)]
            owner = lax.div(partner, local)
            place = lax.bitwise_xor(lax.div(owner, 2), line)
            out_ref[s] = held[lax.rem(owner, 2), place, lax.rem(partner, local)]


def join_pieces(pieces, out_ref):
    line = lax.div(lax.axis_index("seq"), 2)
    rows = BLK // len(pieces)
    for k, ref in enumerate(pieces):
        first = lax.bitwise_xor(line, k) * rows
        for s in range(ref.shape[0]):
            out_ref[pl.ds(pl.multiple_of(s * BLK + first, rows), rows)] = ref[s]


def weight_kernel(groups, plan_ref, rewards_ref, lengths_ref, grad_ref, prompt_ref, out_ref, prompt_out):
    prompt_out[...] = prompt_ref[...]
    me = lax.axis_index("seq")
    local = grad_ref.shape[0] // BLK
    reward_sum = rewards_ref[0, 0]
    for r in range(1, RESP):
        reward_sum = reward_sum + rewards_ref[0, r]
    mean = reward_sum * (1.0 / RESP)
    row = lax.broadcasted_iota(jnp.int32, (BLK, 1), 0)
    for s in range(local):
        block = plan_ref[0, me * local + s]
        response = lax.div(block, NB)
        first = lax.rem(block, NB) * BLK
        scaled = (rewards_ref[0, response] - mean) * (LOSS_SCALE * groups * RESP * NB * BLK)
        weight = jnp.where(row + first < lengths_ref[0, response], scaled, 0.0)
        rows = slice(s * BLK, (s + 1) * BLK)
        out_ref[rows] = (grad_ref[rows].astype(F32) * weight).astype(BF16)


def head_tiles(q_ref):
    halves = q_ref.shape[0] // TILE
    return [
        (h * halves + r, r, slice(r * TILE, (r + 1) * TILE), slice(h * BLK, (h + 1) * BLK))
        for h in range(q_ref.shape[1] // BLK)
        for r in range(halves)
    ]


KEYS = slice(0, BLK)
VALUES = slice(BLK, 2 * BLK)


def block_rows(ref, j):
    rows = slice(j * BLK, (j + 1) * BLK)
    heads = ref.shape[1] // BLK
    return jnp.concatenate([ref[rows, h * BLK : (h + 1) * BLK] for h in range(heads)], axis=0)


def block_seen(plan_ref, j, local, heads):
    if plan_ref is None:
        key = lax.broadcasted_iota(jnp.int32, (BLK, BLK), 0)
        row = lax.broadcasted_iota(jnp.int32, (BLK, BLK), 1)
        return jnp.concatenate([key <= row] * heads, axis=1)
    me = lax.axis_index("seq")
    odd = lax.rem(plan_ref[0, me * local + j], NB)
    return jnp.full((BLK, heads * BLK), odd, jnp.int32) > 0


def merged(scale, first, second):
    peak = jnp.maximum(first[0], second[0])
    a, b = jnp.exp2((first[0] - peak) * scale), jnp.exp2((second[0] - peak) * scale)
    return peak, first[1] * a + second[1] * b, first[2] * a + second[2] * b


def score_stats(scale, s, dp):
    peak = jnp.max(s, axis=0, keepdims=True)
    e = jnp.exp2(s * scale - peak * scale)
    return peak, jnp.sum(e, axis=0, keepdims=True), jnp.sum(e * dp, axis=0, keepdims=True)


def stats_kernel(scale, shards, own, parts, carried, ordered, *refs):
    refs = list(refs)
    plan_ref = refs.pop(0) if parts else None
    q_ref, w_ref = refs.pop(0), refs.pop(0)
    before = refs.pop(0) if carried else None
    kv = [refs.pop(0) for _ in range(shards)]
    own_ref = refs.pop(0) if own else None
    pieces = [refs.pop(0) for _ in range(parts)]
    refs = refs[ordered:]
    out_ref = refs.pop(0)
    heads, local = q_ref.shape[1] // BLK, q_ref.shape[0] // BLK
    block_stats = None
    if parts:
        own_ref = refs.pop(0)
        join_pieces(pieces, own_ref)
    if own_ref is not None:
        block_stats = []
        for j in range(local):
            pairs = own_ref[j * BLK : (j + 1) * BLK]
            s = dot(pairs[:, KEYS], block_rows(q_ref, j), NT)
            dp = dot(pairs[:, VALUES], block_rows(w_ref, j), NT)
            s = jnp.where(block_seen(plan_ref, j, local, heads), s, BIG_NEGATIVE)
            block_stats.append(score_stats(scale, s, dp))
    for t, r, rows, cols in head_tiles(q_ref):
        q, w = q_ref[rows, cols], w_ref[rows, cols]
        state = None
        if carried:
            state = tuple(before[t, i : i + 1] for i in range(3))
        if block_stats is not None:
            pair = block_stats[2 * r : 2 * r + 2]
            more = tuple(jnp.concatenate([x[i][:, cols] for x in pair], axis=1) for i in range(3))
            state = more if state is None else merged(scale, state, more)
        for ref in kv:
            s, dp = dot(ref[:, KEYS], q, NT), dot(ref[:, VALUES], w, NT)
            if state is None:
                state = score_stats(scale, s, dp)
                continue
            m, l, d = state
            peak = jnp.maximum(m, jnp.max(s, axis=0, keepdims=True))
            shrink = jnp.exp2((m - peak) * scale)
            e = jnp.exp2(s * scale - peak * scale)
            l = l * shrink + jnp.sum(e, axis=0, keepdims=True)
            d = d * shrink + jnp.sum(e * dp, axis=0, keepdims=True)
            state = peak, l, d
        for i in range(3):
            out_ref[t, i : i + 1] = state[i]


def grad_kernel(scale, shards, own, partner, carried, ordered, *refs):
    refs = list(refs)
    plan_ref = refs.pop(0) if partner else None
    q_ref, w_ref, stats_ref = refs.pop(0), refs.pop(0), refs.pop(0)
    before = refs.pop(0) if carried else None
    kv = [refs.pop(0) for _ in range(shards)]
    blocks_ref = refs.pop(0) if own or partner else None
    refs = refs[ordered:]
    dq_ref = refs.pop(0)
    kv_out = refs.pop(0) if shards else None
    kv_sum = refs.pop() if shards else None
    if partner:
        blocks_out, blocks_sum = refs[:partner], refs[partner]
    elif own:
        blocks_sum = refs[0]
    heads, local = q_ref.shape[1] // BLK, q_ref.shape[0] // BLK
    halves = q_ref.shape[0] // TILE
    back = scale / LOG2E

    def factors(rows):
        inverse = 1.0 / rows[1]
        return rows[0] * scale, inverse, rows[2] * inverse

    def grads(s, dp, rows):
        peak, inverse, delta = rows
        p = jnp.exp2(s * scale - peak) * inverse
        return p.astype(BF16), (p * (dp - delta)).astype(BF16)

    def add_queries(dq, rows, cols):
        if carried:
            dq = dq + before[rows, cols]
        dq_ref[rows, cols] = dq

    if blocks_ref is not None:
        for j in range(local):
            place = slice(j * BLK, (j + 1) * BLK)
            lanes = slice((j % 2) * BLK, (j % 2 + 1) * BLK)
            rows = [
                jnp.concatenate(
                    [stats_ref[h * halves + j // 2, i : i + 1, lanes] for h in range(heads)], axis=1
                )
                for i in range(3)
            ]
            q, w = block_rows(q_ref, j), block_rows(w_ref, j)
            keys = blocks_ref[place, KEYS]
            s = jnp.where(block_seen(plan_ref, j, local, heads), dot(keys, q, NT), BIG_NEGATIVE)
            p, ds = grads(s, dot(blocks_ref[place, VALUES], w, NT), factors(rows))
            blocks_sum[place, KEYS] = dot(ds, q, NN) * back
            blocks_sum[place, VALUES] = dot(p, w, NN)
            dq = dot(ds, keys, TN)
            for h in range(heads):
                cols = slice(h * BLK, (h + 1) * BLK)
                add_queries(dq[cols], place, cols)
        if partner:
            write_pieces(blocks_sum, blocks_out)
    if not shards:
        return
    keys = jnp.concatenate([ref[:, KEYS] for ref in kv], axis=0)
    values = jnp.concatenate([ref[:, VALUES] for ref in kv], axis=0)
    for t, r, rows, cols in head_tiles(q_ref):
        q, w = q_ref[rows, cols], w_ref[rows, cols]
        state = factors([stats_ref[t, i : i + 1] for i in range(3)])
        p, ds = grads(dot(keys, q, NT), dot(values, w, NT), state)
        dk, dv = dot(ds, q, NN), dot(p, w, NN)
        if t == 0:
            kv_sum[:, KEYS] = dk
            kv_sum[:, VALUES] = dv
        else:
            kv_sum[:, KEYS] += dk
            kv_sum[:, VALUES] += dv
        add_queries(dot(ds, keys, TN), rows, cols)
    for side, factor in ((KEYS, back), (VALUES, 1.0)):
        kv_out[:, side] = (kv_sum[:, side] * factor).astype(kv_out.dtype)


def join_kernel(count, plan_ref, *refs):
    pieces, out_ref = refs[:count], refs[-1]
    me = lax.axis_index("seq")
    join_pieces(pieces, out_ref)
    local = out_ref.shape[0] // BLK
    for s in range(local):
        rows = slice(s * BLK, (s + 1) * BLK)
        odd = lax.rem(plan_ref[0, me * local + s], NB)
        odd_rows = jnp.full((BLK, 2 * BLK), odd, jnp.int32) > 0
        out_ref[rows] = jnp.where(odd_rows, 0.0, out_ref[rows].astype(F32)).astype(BF16)


def finish_kernel(groups, back, *refs):
    total = jnp.int32(0)
    for ref in refs[:groups]:
        for r in range(RESP):
            total = total + ref[0, r]
    share = 1.0 / jnp.full((1, BLK), total.astype(F32))
    dq_ref, own_ref, back_ref, prompt_ref, dq_out, stream_out, prompt_out = refs[groups:]
    for h in range(dq_ref.shape[1] // BLK):
        cols = slice(h * BLK, (h + 1) * BLK)
        dq_out[:, cols] = (dq_ref[:, cols] * (share * back)).astype(BF16)
    for cols in (KEYS, VALUES):
        stream = own_ref[:, cols] + back_ref[:, cols].astype(F32)
        stream_out[:, cols] = (stream * share).astype(BF16)
        prompt_out[:, cols] = (prompt_ref[:, cols] * share).astype(BF16)


def pick_kernel(per, parts, picked, ordered, *refs):
    out_ref, refs = refs[-1], refs[: len(refs) - 1 - ordered]
    where = []
    for ref in refs[:parts]:
        where += [(ref, i) for i in range(ref.shape[0] // per)]
    for n, i in enumerate(picked):
        ref, at = where[i]
        total = ref[at * per : (at + 1) * per].astype(F32)
        for other in refs[parts:]:
            total = total + other[i * per : (i + 1) * per].astype(F32)
        out_ref[n * per : (n + 1) * per] = total.astype(out_ref.dtype)


def local(query, resp_kv, prompt_kv, grad_out, rewards, lengths, block_order):
    groups = lax.axis_size("grp")
    count = lax.axis_size("seq")
    q, resp, prompt, grad = query[0], resp_kv[0], prompt_kv[0], grad_out[0]
    rows, width = resp.shape
    blocks = rows // BLK
    heads = q.shape[1] // BLK
    line = count // 2
    scale = LOG2E * BLK**-0.5
    piece = jax.ShapeDtypeStruct((blocks, BLK // line, width), BF16)
    stack = jax.ShapeDtypeStruct((line, *piece.shape), BF16)

    def swap(x, axis, k):
        size = lax.axis_size(axis)
        return lax.ppermute(x, axis, [(i, i ^ k) for i in range(size)])

    def along(sent):
        return [sent[0]] + [swap(sent[k], "seq", 2 * k) for k in range(1, line)]

    def gather_line(name, sent, after=()):
        body = partial(stack_kernel, line)
        return call(body, name, stack, [VMEM] * line, along(sent), after=after)

    def deliver(name, mine, after=()):
        other = swap(mine, "seq", 1)
        return call(
            partial(route_kernel, line),
            name + "_route",
            [piece] * line,
            [SMEM, VMEM, VMEM],
            [block_order, mine, other],
            [pltpu.VMEM((2, *stack.shape), BF16), pltpu.SMEM((block_order.shape[1],), jnp.int32)],
            after=after,
        )

    pieces = call(split_kernel, "pairs_split", [piece] * line, [VMEM], [resp])
    weighted, prompt_on = call(
        partial(weight_kernel, groups),
        "weight_rows",
        [jax.ShapeDtypeStruct(grad.shape, BF16), jax.ShapeDtypeStruct(prompt.shape, BF16)],
        [SMEM, SMEM, SMEM, VMEM, VMEM],
        [block_order, rewards, lengths, grad, prompt],
    )
    mine = gather_line("pairs_stack", pieces, after=[weighted])
    stats_shape = jax.ShapeDtypeStruct((heads * rows // TILE, 8, TILE), F32)

    def stats(name, before, kv, own=None, parts=(), after=(), beside=False):
        args = [block_order] if parts else []
        specs = [SMEM] * len(args)
        args += [q, weighted] + ([before] if before is not None else []) + list(kv)
        args += ([own] if own is not None else []) + list(parts)
        specs += [VMEM] * (len(args) - len(specs))
        out = [stats_shape]
        if parts:
            out.append(jax.ShapeDtypeStruct(resp.shape, BF16))
        body = partial(
            stats_kernel,
            scale,
            len(kv),
            own is not None,
            len(parts),
            before is not None,
            len(after),
        )
        return call(body, name, out, specs, args, after=after, beside=beside)

    (state,) = stats("stats_own", None, [prompt_on], own=resp, after=[mine])
    routed = deliver("pairs", mine, after=[state])
    arrived = along(routed)

    def held_back(x, after):
        same = jax.ShapeDtypeStruct(x.shape, x.dtype)
        return call(pass_kernel, "pass_on", same, [VMEM], [x], after=[after])

    column = {0: prompt_on}
    bit = count // 2
    while bit > 1:
        column.update({k ^ bit: swap(x, "seq", bit) for k, x in column.items()})
        if bit == count // 2 or bit == 2:
            column[bit] = held_back(column[bit], state)
        bit //= 2
    early = [k for k in column if not k & 2 or k == 2]
    late = [k for k in column if k not in early]
    across = {k: swap(column[k], "seq", 1) for k in early}
    coming = [x for k, x in column.items() if k] + [across[k] for k in early]
    (state,) = stats("stats_prompt", state, coming[:2], after=[routed[0]])
    across.update({k: swap(held_back(column[k], state), "seq", 1) for k in late})
    coming = coming[2:]
    while len(coming) > 2:
        (state,) = stats("stats_prompt", state, coming[:2])
        coming = coming[2:]
    state, partner = stats("stats_partner", state, coming, parts=arrived, beside=True)
    (state,) = stats("stats_last", state, [across[k] for k in late])

    def grads(name, before, kv, own=None, part=None, kind=BF16, after=(), beside=False):
        args = [block_order] if part is not None else []
        specs = [SMEM] * len(args)
        args += [q, weighted, state] + ([before] if before is not None else [])
        args += list(kv) + [x for x in (own, part) if x is not None]
        specs += [VMEM] * (len(args) - len(specs))
        keys = sum(x.shape[0] for x in kv)
        out = [jax.ShapeDtypeStruct(q.shape, F32)]
        out += [jax.ShapeDtypeStruct((keys, width), kind)] if kv else []
        scratch = [pltpu.VMEM((keys, width), F32)] if kv else []
        if own is not None:
            out.append(jax.ShapeDtypeStruct(resp.shape, F32))
        if part is not None:
            out += [piece] * line
            scratch.append(pltpu.VMEM(resp.shape, F32))
        body = partial(
            grad_kernel,
            scale,
            len(kv),
            own is not None,
            line if part is not None else 0,
            before is not None,
            len(after),
        )
        return call(body, name, out, specs, args, scratch, after=after, beside=beside)

    per = prompt.shape[0]

    def pick(name, parts, extra, picked, kind, after=(), beside=False):
        args = [*parts, *extra]
        return call(
            partial(pick_kernel, per, len(parts), tuple(picked), len(after)),
            name,
            jax.ShapeDtypeStruct((per * len(picked), width), kind),
            [VMEM] * len(args),
            args,
            after=after,
            beside=beside,
        )

    near = [k for k in column if k & 2]
    rest = [k for k in column if not k & 2]
    dq, *terms = grads("grads_partner", None, [], part=partner)
    dq, far_near = grads("grads_across", dq, [across[k] for k in near])
    mine = gather_line("terms_stack", terms, after=[far_near])
    far_near = swap(far_near, "seq", 1)
    dq, sums = grads("grads_near", dq, [column[k] for k in near], kind=F32, after=[mine], beside=True)
    dq, far_rest = grads("grads_across", dq, [across[k] for k in rest])
    sums = pick("sum_near", [sums], [far_near], range(len(near)), BF16, after=[far_rest])
    far_rest = swap(far_rest, "seq", 1)
    dq, sent = grads("grads_rest", dq, [column[k] for k in rest], kind=F32, after=[sums])
    sums = swap(sums, "seq", 2)
    routed = deliver("terms", mine, after=[sent])
    returned = along(routed)
    sums_on = call(
        pass_kernel,
        "pass_sums",
        jax.ShapeDtypeStruct(sums.shape, BF16),
        [VMEM],
        [sums],
        after=[routed[0]],
        beside=True,
    )
    held, parts, extra, order = rest, [sent], [far_rest, sums_on], []
    bit = 4
    while bit < count:
        keep = [i for i, k in enumerate(held) if not k & bit]
        send = [i for i, k in enumerate(held) if k & bit]
        leaving = pick("sum_far", parts, extra, send, BF16, after=order)
        kept = pick("sum_kept", parts, extra, keep, F32)
        held, parts, extra, order = [held[i] for i in keep], [kept], [swap(leaving, "seq", bit)], []
        if bit == 4:
            dq, own_terms = grads("grads_own", dq, [], own=resp, after=[leaving], beside=False)
            lengths_on = call(
                pass_kernel,
                "pass_lengths",
                jax.ShapeDtypeStruct(lengths.shape, jnp.int32),
                [VMEM],
                [lengths],
                after=[own_terms],
            )
            joined = call(
                partial(join_kernel, line),
                "join_terms",
                jax.ShapeDtypeStruct(resp.shape, BF16),
                [SMEM] + [VMEM] * line,
                [block_order, *returned],
                after=[own_terms],
            )
        bit *= 2
    lengths_all = [lengths] + [swap(lengths_on, "grp", k) for k in range(1, groups)]
    prompt_sum = pick("sum_prompt", parts, extra, [0], F32, after=[joined], beside=True)
    grad_query, grad_stream, grad_prompt = call(
        partial(finish_kernel, groups, scale / LOG2E),
        "over_count",
        [jax.ShapeDtypeStruct(x.shape, BF16) for x in (q, resp, prompt)],
        [SMEM] * groups + [VMEM] * 4,
        [*lengths_all, dq, own_terms, joined, prompt_sum],
    )
    return grad_query[None], grad_stream[None], grad_prompt[None]


def solution(mesh):
    in_specs = (
        P("grp", "seq", None),
        P("grp", "seq", None),
        P("grp", "seq", None),
        P("grp", "seq", None),
        P("grp", None),
        P("grp", None),
        P("grp", None),
    )
    out_specs = (P("grp", "seq", None), P("grp", "seq", None), P("grp", "seq", None))
    return jax.shard_map(local, mesh=mesh, in_specs=in_specs, out_specs=out_specs, check_vma=False)
```

```python
from functools import partial

import jax
import jax.numpy as jnp
from jax import lax
from jax.experimental import pallas as pl
from jax.experimental.pallas import tpu as pltpu
from jax.sharding import PartitionSpec as P

RESP = 16
BLK = 128
NB = 2
LOSS_SCALE = 32.0
BIG_NEGATIVE = -1e30
COVER = 7 * 10**9
LOG2E = 1.4426950408889634

F32 = jnp.float32
BF16 = jnp.bfloat16
NT = (((1,), (1,)), ((), ()))
NN = (((1,), (0,)), ((), ()))
TILE = 2 * BLK
VMEM = pl.BlockSpec(memory_space=pltpu.VMEM)
SMEM = pl.BlockSpec(memory_space=pltpu.SMEM)
ANY = pl.BlockSpec(memory_space=pl.ANY)


def dot(a, b, dims):
    return lax.dot_general(a, b, dims, preferred_element_type=F32)


def call(kernel, name, out_shape, specs, args, scratch=(), after=(), beside=False):
    specs, args = [*specs, *[ANY] * len(after)], [*args, *after]
    return pl.pallas_call(
        kernel,
        name=name,
        out_shape=out_shape,
        in_specs=specs,
        out_specs=jax.tree.map(lambda _: VMEM, out_shape),
        scratch_shapes=list(scratch),
        compiler_params=pltpu.CompilerParams(vmem_limit_bytes=24 * 2**20),
        cost_estimate=pl.CostEstimate(flops=COVER * beside, bytes_accessed=0, transcendentals=0),
    )(*args)


def write_pieces(pairs_ref, out_refs):
    line = lax.div(lax.axis_index("seq"), 2)
    rows = BLK // len(out_refs)
    for k, out_ref in enumerate(out_refs):
        first = lax.bitwise_xor(line, k) * rows
        for s in range(out_ref.shape[0]):
            place = pl.ds(pl.multiple_of(s * BLK + first, rows), rows)
            out_ref[s] = pairs_ref[place].astype(BF16)


def split_kernel(kv_ref, *out_refs):
    write_pieces(kv_ref, out_refs)


def stack_kernel(count, *refs):
    for k in range(count):
        refs[-1][k] = refs[k][...]


def pass_kernel(x_ref, after_ref, out_ref):
    out_ref[...] = x_ref[...]


def add_kernel(x_ref, y_ref, after_ref, out_ref):
    out_ref[...] = x_ref[...] + y_ref[...]


def route_kernel(count, plan_ref, mine_ref, other_ref, *refs):
    outs, held, inverse = refs[len(refs) - 2 - count : -2], refs[-2], refs[-1]
    me = lax.axis_index("seq")
    line, side = lax.div(me, 2), lax.rem(me, 2)
    held[side] = mine_ref[...]
    held[1 - side] = other_ref[...]
    local = mine_ref.shape[1]
    for j in range(plan_ref.shape[1]):
        inverse[plan_ref[0, j]] = j
    for k, out_ref in enumerate(outs):
        device = lax.bitwise_xor(line, k) * 2 + side
        for s in range(local):
            partner = inverse[lax.bitwise_xor(plan_ref[0, device * local + s], 1)]
            owner = lax.div(partner, local)
            place = lax.bitwise_xor(lax.div(owner, 2), line)
            out_ref[s] = held[lax.rem(owner, 2), place, lax.rem(partner, local)]


def join_pieces(pieces, out_ref, start=0):
    line = lax.div(lax.axis_index("seq"), 2)
    rows = BLK // len(pieces)
    for k, ref in enumerate(pieces):
        place = lax.bitwise_xor(line, k) * rows
        for s in range(out_ref.shape[0] // BLK):
            piece = ref[s] if len(ref.shape) == 3 else ref[start + s * rows : start + (s + 1) * rows]
            out_ref[pl.ds(pl.multiple_of(s * BLK + place, rows), rows)] = piece


def weight_kernel(groups, plan_ref, rewards_ref, lengths_ref, grad_ref, prompt_ref, out_ref, prompt_out):
    prompt_out[...] = prompt_ref[...]
    me = lax.axis_index("seq")
    local = grad_ref.shape[0] // BLK
    reward_sum = rewards_ref[0, 0]
    for r in range(1, RESP):
        reward_sum = reward_sum + rewards_ref[0, r]
    mean = reward_sum * (1.0 / RESP)
    row = lax.broadcasted_iota(jnp.int32, (BLK, 1), 0)
    for s in range(local):
        block = plan_ref[0, me * local + s]
        response = lax.div(block, NB)
        first = lax.rem(block, NB) * BLK
        scaled = (rewards_ref[0, response] - mean) * (LOSS_SCALE * groups * RESP * NB * BLK)
        weight = jnp.where(row + first < lengths_ref[0, response], scaled, 0.0)
        rows = slice(s * BLK, (s + 1) * BLK)
        out_ref[rows] = (grad_ref[rows].astype(F32) * weight).astype(BF16)


def head_tiles(q_ref):
    halves = q_ref.shape[0] // TILE
    return [
        (h * halves + r, r, slice(r * TILE, (r + 1) * TILE), slice(h * BLK, (h + 1) * BLK))
        for h in range(q_ref.shape[1] // BLK)
        for r in range(halves)
    ]


KEYS = slice(0, BLK)
VALUES = slice(BLK, 2 * BLK)


def block_rows(ref, j):
    rows = slice(j * BLK, (j + 1) * BLK)
    heads = ref.shape[1] // BLK
    return jnp.concatenate([ref[rows, h * BLK : (h + 1) * BLK] for h in range(heads)], axis=0)


def block_seen(plan_ref, j, local, heads):
    if plan_ref is None:
        key = lax.broadcasted_iota(jnp.int32, (BLK, BLK), 0)
        row = lax.broadcasted_iota(jnp.int32, (BLK, BLK), 1)
        return jnp.concatenate([key <= row] * heads, axis=1)
    me = lax.axis_index("seq")
    odd = lax.rem(plan_ref[0, me * local + j], NB)
    return jnp.full((BLK, heads * BLK), odd, jnp.int32) > 0


def merged(scale, first, second):
    peak = jnp.maximum(first[0], second[0])
    a, b = jnp.exp2((first[0] - peak) * scale), jnp.exp2((second[0] - peak) * scale)
    return peak, first[1] * a + second[1] * b, first[2] * a + second[2] * b


def score_stats(scale, s, dp):
    peak = jnp.max(s, axis=0, keepdims=True)
    e = jnp.exp2(s * scale - peak * scale)
    return peak, jnp.sum(e, axis=0, keepdims=True), jnp.sum(e * dp, axis=0, keepdims=True)


def stats_kernel(scale, shards, own, parts, carried, ordered, *refs):
    refs = list(refs)
    plan_ref = refs.pop(0) if parts else None
    q_ref, w_ref = refs.pop(0), refs.pop(0)
    before = refs.pop(0) if carried else None
    kv = [refs.pop(0) for _ in range(shards)]
    own_ref = refs.pop(0) if own else None
    pieces = [refs.pop(0) for _ in range(parts)]
    refs = refs[ordered:]
    out_ref = refs.pop(0)
    heads, local = q_ref.shape[1] // BLK, q_ref.shape[0] // BLK
    block_stats = None
    if parts:
        own_ref = refs.pop(0)
        join_pieces(pieces, own_ref)
    if own_ref is not None:
        block_stats = []
        for j in range(local):
            pairs = own_ref[j * BLK : (j + 1) * BLK]
            s = dot(pairs[:, KEYS], block_rows(q_ref, j), NT)
            dp = dot(pairs[:, VALUES], block_rows(w_ref, j), NT)
            s = jnp.where(block_seen(plan_ref, j, local, heads), s, BIG_NEGATIVE)
            block_stats.append(score_stats(scale, s, dp))
    for t, r, rows, cols in head_tiles(q_ref):
        q, w = q_ref[rows, cols], w_ref[rows, cols]
        state = None
        if carried:
            state = tuple(before[t, i : i + 1] for i in range(3))
        if block_stats is not None:
            pair = block_stats[2 * r : 2 * r + 2]
            more = tuple(jnp.concatenate([x[i][:, cols] for x in pair], axis=1) for i in range(3))
            state = more if state is None else merged(scale, state, more)
        for ref in kv:
            s, dp = dot(ref[:, KEYS], q, NT), dot(ref[:, VALUES], w, NT)
            if state is None:
                state = score_stats(scale, s, dp)
                continue
            m, l, d = state
            peak = jnp.maximum(m, jnp.max(s, axis=0, keepdims=True))
            shrink = jnp.exp2((m - peak) * scale)
            e = jnp.exp2(s * scale - peak * scale)
            l = l * shrink + jnp.sum(e, axis=0, keepdims=True)
            d = d * shrink + jnp.sum(e * dp, axis=0, keepdims=True)
            state = peak, l, d
        for i in range(3):
            out_ref[t, i : i + 1] = state[i]


def grad_kernel(scale, shards, own, partner, carried, ordered, *refs):
    refs = list(refs)
    plan_ref = refs.pop(0) if partner else None
    q_ref, w_ref, stats_ref = refs.pop(0), refs.pop(0), refs.pop(0)
    before = refs.pop(0) if carried else None
    kv = [refs.pop(0) for _ in range(shards)]
    blocks_ref = refs.pop(0) if own or partner else None
    refs = refs[ordered:]
    dq_ref = refs.pop(0)
    kv_out = refs.pop(0) if shards else None
    kv_sum = refs.pop() if shards else None
    if partner:
        blocks_out, blocks_sum = refs[:partner], refs[partner]
    elif own:
        blocks_sum = refs[0]
    heads, local = q_ref.shape[1] // BLK, q_ref.shape[0] // BLK
    halves = q_ref.shape[0] // TILE
    back = scale / LOG2E

    def factors(rows):
        inverse = 1.0 / rows[1]
        return rows[0] * scale, inverse, rows[2] * inverse

    def grads(s, dp, rows):
        peak, inverse, delta = rows
        p = jnp.exp2(s * scale - peak) * inverse
        return p.astype(BF16), (p * (dp - delta)).astype(BF16)

    def add_queries(dq, rows, cols):
        if carried:
            dq = dq + before[cols, rows]
        dq_ref[cols, rows] = dq

    if blocks_ref is not None:
        for j in range(local):
            place = slice(j * BLK, (j + 1) * BLK)
            lanes = slice((j % 2) * BLK, (j % 2 + 1) * BLK)
            rows = [
                jnp.concatenate(
                    [stats_ref[h * halves + j // 2, i : i + 1, lanes] for h in range(heads)], axis=1
                )
                for i in range(3)
            ]
            q, w = block_rows(q_ref, j), block_rows(w_ref, j)
            keys = blocks_ref[place, KEYS]
            s = jnp.where(block_seen(plan_ref, j, local, heads), dot(keys, q, NT), BIG_NEGATIVE)
            p, ds = grads(s, dot(blocks_ref[place, VALUES], w, NT), factors(rows))
            blocks_sum[place, KEYS] = dot(ds, q, NN) * back
            blocks_sum[place, VALUES] = dot(p, w, NN)
            dq = dot(keys.T, ds, NN)
            for h in range(heads):
                cols = slice(h * BLK, (h + 1) * BLK)
                add_queries(dq[:, cols], place, cols)
        if partner:
            write_pieces(blocks_sum, blocks_out)
    if not shards:
        return
    keys = jnp.concatenate([ref[:, KEYS] for ref in kv], axis=0)
    values = jnp.concatenate([ref[:, VALUES] for ref in kv], axis=0)
    turned = keys.T
    for t, r, rows, cols in head_tiles(q_ref):
        q, w = q_ref[rows, cols], w_ref[rows, cols]
        state = factors([stats_ref[t, i : i + 1] for i in range(3)])
        p, ds = grads(dot(keys, q, NT), dot(values, w, NT), state)
        dk, dv = dot(ds, q, NN), dot(p, w, NN)
        if t == 0:
            kv_sum[:, KEYS] = dk
            kv_sum[:, VALUES] = dv
        else:
            kv_sum[:, KEYS] += dk
            kv_sum[:, VALUES] += dv
        add_queries(dot(turned, ds, NN), rows, cols)
    for side, factor in ((KEYS, back), (VALUES, 1.0)):
        kv_out[:, side] = (kv_sum[:, side] * factor).astype(kv_out.dtype)


def finish_kernel(back, start, plan_ref, lengths_ref, *refs):
    total = jnp.int32(0)
    for r in range(RESP):
        total = total + lengths_ref[0, r]
    share = 1.0 / jnp.full((1, BLK), total.astype(F32))
    (dq_ref, own_ref, prompt_ref), pieces = refs[:3], refs[3:-4]
    dq_out, stream_out, prompt_out, held = refs[-4:]
    join_pieces(pieces, held, start)
    me = lax.axis_index("seq")
    local = own_ref.shape[0] // BLK
    for h in range(dq_ref.shape[0] // BLK):
        cols = slice(h * BLK, (h + 1) * BLK)
        dq_out[:, cols] = (dq_ref[cols, :] * (share[:, :1] * back)).astype(BF16).T
    for cols in (KEYS, VALUES):
        for s in range(local):
            rows = slice(s * BLK, (s + 1) * BLK)
            odd = lax.rem(plan_ref[0, me * local + s], NB)
            odd_rows = jnp.full((BLK, BLK), odd, jnp.int32) > 0
            stream = own_ref[rows, cols] + jnp.where(odd_rows, 0.0, held[rows, cols].astype(F32))
            stream_out[rows, cols] = (stream * share).astype(BF16)
        prompt_out[:, cols] = (prompt_ref[:, cols] * share).astype(BF16)


def pick_kernel(per, parts, picked, joined, ordered, *refs):
    out_ref, refs = refs[-1], refs[: len(refs) - 1 - ordered]
    if joined:
        piece, refs = refs[-1], refs[:-1]
        first, rows = len(picked) * per, piece.shape[1]
        for s in range(piece.shape[0]):
            out_ref[first + s * rows : first + (s + 1) * rows] = piece[s]
    where = []
    for ref in refs[:parts]:
        where += [(ref, i) for i in range(ref.shape[0] // per)]
    for n, i in enumerate(picked):
        ref, at = where[i]
        total = ref[at * per : (at + 1) * per].astype(F32)
        for other in refs[parts:]:
            total = total + other[i * per : (i + 1) * per].astype(F32)
        out_ref[n * per : (n + 1) * per] = total.astype(out_ref.dtype)


def local(query, resp_kv, prompt_kv, grad_out, rewards, lengths, block_order):
    groups = lax.axis_size("grp")
    count = lax.axis_size("seq")
    q, resp, prompt, grad = query[0], resp_kv[0], prompt_kv[0], grad_out[0]
    rows, width = resp.shape
    blocks = rows // BLK
    heads = q.shape[1] // BLK
    line = count // 2
    scale = LOG2E * BLK**-0.5
    piece = jax.ShapeDtypeStruct((blocks, BLK // line, width), BF16)
    stack = jax.ShapeDtypeStruct((line, *piece.shape), BF16)

    def swap(x, axis, k):
        size = lax.axis_size(axis)
        return lax.ppermute(x, axis, [(i, i ^ k) for i in range(size)])

    def along(sent):
        return [sent[0]] + [swap(sent[k], "seq", 2 * k) for k in range(1, line)]

    def gather_line(name, sent, after=()):
        body = partial(stack_kernel, line)
        return call(body, name, stack, [VMEM] * line, along(sent), after=after)

    def deliver(name, mine, after=()):
        other = swap(mine, "seq", 1)
        return call(
            partial(route_kernel, line),
            name + "_route",
            [piece] * line,
            [SMEM, VMEM, VMEM],
            [block_order, mine, other],
            [pltpu.VMEM((2, *stack.shape), BF16), pltpu.SMEM((block_order.shape[1],), jnp.int32)],
            after=after,
        )

    pieces = call(split_kernel, "pairs_split", [piece] * line, [VMEM], [resp])
    weighted, prompt_on = call(
        partial(weight_kernel, groups),
        "weight_rows",
        [jax.ShapeDtypeStruct(grad.shape, BF16), jax.ShapeDtypeStruct(prompt.shape, BF16)],
        [SMEM, SMEM, SMEM, VMEM, VMEM],
        [block_order, rewards, lengths, grad, prompt],
    )
    mine = gather_line("pairs_stack", pieces, after=[weighted])
    stats_shape = jax.ShapeDtypeStruct((heads * rows // TILE, 8, TILE), F32)

    def stats(name, before, kv, own=None, parts=(), after=(), beside=False):
        args = [block_order] if parts else []
        specs = [SMEM] * len(args)
        args += [q, weighted] + ([before] if before is not None else []) + list(kv)
        args += ([own] if own is not None else []) + list(parts)
        specs += [VMEM] * (len(args) - len(specs))
        out = [stats_shape]
        if parts:
            out.append(jax.ShapeDtypeStruct(resp.shape, BF16))
        body = partial(
            stats_kernel,
            scale,
            len(kv),
            own is not None,
            len(parts),
            before is not None,
            len(after),
        )
        return call(body, name, out, specs, args, after=after, beside=beside)

    (state,) = stats("stats_own", None, [prompt_on], own=resp, after=[mine])
    routed = deliver("pairs", mine, after=[state])
    arrived = along(routed)

    def held_back(x, after):
        same = jax.ShapeDtypeStruct(x.shape, x.dtype)
        return call(pass_kernel, "pass_on", same, [VMEM], [x], after=[after])

    column = {0: prompt_on}
    bit = count // 2
    while bit > 1:
        column.update({k ^ bit: swap(x, "seq", bit) for k, x in column.items()})
        if bit == count // 2 or bit == 2:
            column[bit] = held_back(column[bit], state)
        bit //= 2
    early = [k for k in column if not k & 2 or k == 2]
    late = [k for k in column if k not in early]
    across = {k: swap(column[k] if k else prompt_on, "seq", 1) for k in early}
    coming = [x for k, x in column.items() if k] + [across[k] for k in early]
    (state,) = stats("stats_prompt", state, coming[:2], after=[routed[0]])
    across.update({k: swap(held_back(column[k], state), "seq", 1) for k in late})
    coming = coming[2:]
    while len(coming) > 2:
        (state,) = stats("stats_prompt", state, coming[:2])
        coming = coming[2:]
    state, partner = stats("stats_partner", state, coming, parts=arrived, beside=True)
    (state,) = stats("stats_last", state, [across[k] for k in late])

    def grads(name, before, kv, own=None, part=None, kind=BF16, after=(), beside=False):
        args = [block_order] if part is not None else []
        specs = [SMEM] * len(args)
        args += [q, weighted, state] + ([before] if before is not None else [])
        args += list(kv) + [x for x in (own, part) if x is not None]
        specs += [VMEM] * (len(args) - len(specs))
        keys = sum(x.shape[0] for x in kv)
        out = [jax.ShapeDtypeStruct(q.shape[::-1], F32)]
        out += [jax.ShapeDtypeStruct((keys, width), kind)] if kv else []
        scratch = [pltpu.VMEM((keys, width), F32)] if kv else []
        if own is not None:
            out.append(jax.ShapeDtypeStruct(resp.shape, F32))
        if part is not None:
            out += [piece] * line
            scratch.append(pltpu.VMEM(resp.shape, F32))
        body = partial(
            grad_kernel,
            scale,
            len(kv),
            own is not None,
            line if part is not None else 0,
            before is not None,
            len(after),
        )
        return call(body, name, out, specs, args, scratch, after=after, beside=beside)

    per = prompt.shape[0]

    def pick(name, parts, extra, picked, kind, joined=(), after=(), beside=False):
        args = [*parts, *extra, *joined]
        height = per * len(picked) + sum(x.shape[0] * x.shape[1] for x in joined)
        return call(
            partial(pick_kernel, per, len(parts), tuple(picked), len(joined), len(after)),
            name,
            jax.ShapeDtypeStruct((height, width), kind),
            [VMEM] * len(args),
            args,
            after=after,
            beside=beside,
        )

    near = [k for k in column if k & 2]
    rest = [k for k in column if not k & 2]
    dq, *terms = grads("grads_partner", None, [], part=partner)
    dq, far_near = grads("grads_across", dq, [across[k] for k in near])
    mine = gather_line("terms_stack", terms, after=[far_near])
    far_near = swap(far_near, "seq", 1)
    dq, sums = grads("grads_near", dq, [column[k] for k in near], kind=F32, after=[mine], beside=True)
    dq, far_rest = grads("grads_across", dq, [across[k] for k in rest])
    sums = pick("sum_near", [sums], [far_near], range(len(near)), BF16, after=[far_rest])
    far_rest = swap(far_rest, "seq", 1)
    as_lengths = jax.ShapeDtypeStruct(lengths.shape, jnp.int32)

    def added(x, step, after):
        args = [x, swap(x, "grp", step)]
        return call(add_kernel, "add_lengths", as_lengths, [VMEM] * 2, args, after=[after])

    total = call(pass_kernel, "pass_lengths", as_lengths, [VMEM], [lengths], after=[sums])
    dq, sent = grads("grads_rest", dq, [column[k] for k in rest], kind=F32, after=[sums])
    sums = swap(sums, "seq", 2)
    step = 1
    if step < groups:
        total, step = added(total, step, sent), 2
    routed = deliver("terms", mine, after=[sent])
    returned = {k: routed[k] if k == 0 else swap(routed[k], "seq", 2 * k) for k in range(line) if k != 2}
    sums_on = call(
        pass_kernel,
        "pass_sums",
        jax.ShapeDtypeStruct(sums.shape, BF16),
        [VMEM],
        [sums],
        after=[routed[0]],
        beside=True,
    )
    held, parts, extra, order = rest, [sent], [far_rest, sums_on], []
    bit = 4
    while bit < count:
        keep = [i for i, k in enumerate(held) if not k & bit]
        send = [i for i, k in enumerate(held) if k & bit]
        joined = [routed[2]] if bit == 4 else []
        leaving = pick("sum_far", parts, extra, send, BF16, joined=joined, after=order)
        kept = pick("sum_kept", parts, extra, keep, F32)
        held, parts, extra, order = [held[i] for i in keep], [kept], [swap(leaving, "seq", bit)], []
        if bit == 4:
            returned[2], start = extra[0], per * len(send)
            dq, own_terms = grads("grads_own", dq, [], own=resp, after=[leaving])
        bit *= 2
    while step < groups:
        total = added(total, step, own_terms)
        step *= 2
    prompt_sum = pick("sum_prompt", parts, extra, [0], F32, after=[own_terms])
    grad_query, grad_stream, grad_prompt = call(
        partial(finish_kernel, scale / LOG2E, start),
        "over_count",
        [jax.ShapeDtypeStruct(x.shape, BF16) for x in (q, resp, prompt)],
        [SMEM] * 2 + [VMEM] * (3 + line),
        [block_order, total, dq, own_terms, prompt_sum, *[returned[k] for k in range(line)]],
        [pltpu.VMEM(resp.shape, BF16)],
    )
    return grad_query[None], grad_stream[None], grad_prompt[None]


def solution(mesh):
    in_specs = (
        P("grp", "seq", None),
        P("grp", "seq", None),
        P("grp", "seq", None),
        P("grp", "seq", None),
        P("grp", None),
        P("grp", None),
        P("grp", None),
    )
    out_specs = (P("grp", "seq", None), P("grp", "seq", None), P("grp", "seq", None))
    return jax.shard_map(local, mesh=mesh, in_specs=in_specs, out_specs=out_specs, check_vma=False)
```

```python
from functools import partial

import jax
import jax.numpy as jnp
from jax import lax
from jax.experimental import pallas as pl
from jax.experimental.pallas import tpu as pltpu
from jax.sharding import PartitionSpec as P

RESP = 16
BLK = 128
NB = 2
LOSS_SCALE = 32.0
BIG_NEGATIVE = -1e30
COVER = 7 * 10**9
LOG2E = 1.4426950408889634

F32 = jnp.float32
BF16 = jnp.bfloat16
NT = (((1,), (1,)), ((), ()))
NN = (((1,), (0,)), ((), ()))
TILE = 2 * BLK
VMEM = pl.BlockSpec(memory_space=pltpu.VMEM)
SMEM = pl.BlockSpec(memory_space=pltpu.SMEM)
ANY = pl.BlockSpec(memory_space=pl.ANY)


def dot(a, b, dims):
    return lax.dot_general(a, b, dims, preferred_element_type=F32)


def call(kernel, name, out_shape, specs, args, scratch=(), after=(), beside=False, out_spec=VMEM):
    specs, args = [*specs, *[ANY] * len(after)], [*args, *after]
    return pl.pallas_call(
        kernel,
        name=name,
        out_shape=out_shape,
        in_specs=specs,
        out_specs=jax.tree.map(lambda _: out_spec, out_shape),
        scratch_shapes=list(scratch),
        compiler_params=pltpu.CompilerParams(vmem_limit_bytes=24 * 2**20),
        cost_estimate=pl.CostEstimate(flops=COVER * beside, bytes_accessed=0, transcendentals=0),
    )(*args)


def write_pieces(pairs_ref, out_refs):
    line = lax.div(lax.axis_index("seq"), 2)
    rows = BLK // len(out_refs)
    for k, out_ref in enumerate(out_refs):
        first = lax.bitwise_xor(line, k) * rows
        for s in range(out_ref.shape[0]):
            place = pl.ds(pl.multiple_of(s * BLK + first, rows), rows)
            out_ref[s] = pairs_ref[place].astype(BF16)


def split_kernel(kv_ref, *out_refs):
    write_pieces(kv_ref, out_refs)


def stack_kernel(count, *refs):
    for k in range(count):
        refs[-1][k] = refs[k][...]


def pass_kernel(x_ref, after_ref, out_ref):
    out_ref[...] = x_ref[...]


def add_kernel(x_ref, y_ref, after_ref, out_ref):
    out_ref[...] = x_ref[...] + y_ref[...]


def route_kernel(count, plan_ref, mine_ref, other_ref, *refs):
    outs, held, inverse = refs[len(refs) - 2 - count : -2], refs[-2], refs[-1]
    me = lax.axis_index("seq")
    line, side = lax.div(me, 2), lax.rem(me, 2)
    held[side] = mine_ref[...]
    held[1 - side] = other_ref[...]
    local = mine_ref.shape[1]
    for j in range(plan_ref.shape[1]):
        inverse[plan_ref[0, j]] = j
    for k, out_ref in enumerate(outs):
        device = lax.bitwise_xor(line, k) * 2 + side
        for s in range(local):
            partner = inverse[lax.bitwise_xor(plan_ref[0, device * local + s], 1)]
            owner = lax.div(partner, local)
            place = lax.bitwise_xor(lax.div(owner, 2), line)
            out_ref[s] = held[lax.rem(owner, 2), place, lax.rem(partner, local)]


def join_pieces(pieces, out_ref, start=0):
    line = lax.div(lax.axis_index("seq"), 2)
    rows = BLK // len(pieces)
    for k, ref in enumerate(pieces):
        place = lax.bitwise_xor(line, k) * rows
        for s in range(out_ref.shape[0] // BLK):
            piece = ref[s] if len(ref.shape) == 3 else ref[start + s * rows : start + (s + 1) * rows]
            out_ref[pl.ds(pl.multiple_of(s * BLK + place, rows), rows)] = piece


def weight_kernel(groups, plan_ref, rewards_ref, lengths_ref, grad_ref, prompt_ref, out_ref, prompt_out):
    prompt_out[...] = prompt_ref[...]
    me = lax.axis_index("seq")
    local = grad_ref.shape[0] // BLK
    reward_sum = rewards_ref[0, 0]
    for r in range(1, RESP):
        reward_sum = reward_sum + rewards_ref[0, r]
    mean = reward_sum * (1.0 / RESP)
    row = lax.broadcasted_iota(jnp.int32, (BLK, 1), 0)
    for s in range(local):
        block = plan_ref[0, me * local + s]
        response = lax.div(block, NB)
        first = lax.rem(block, NB) * BLK
        scaled = (rewards_ref[0, response] - mean) * (LOSS_SCALE * groups * RESP * NB * BLK)
        weight = jnp.where(row + first < lengths_ref[0, response], scaled, 0.0)
        rows = slice(s * BLK, (s + 1) * BLK)
        out_ref[rows] = (grad_ref[rows].astype(F32) * weight).astype(BF16)


def head_tiles(q_ref):
    halves = q_ref.shape[0] // TILE
    return [
        (h * halves + r, r, slice(r * TILE, (r + 1) * TILE), slice(h * BLK, (h + 1) * BLK))
        for h in range(q_ref.shape[1] // BLK)
        for r in range(halves)
    ]


KEYS = slice(0, BLK)
VALUES = slice(BLK, 2 * BLK)


def block_rows(ref, j):
    rows = slice(j * BLK, (j + 1) * BLK)
    heads = ref.shape[1] // BLK
    return jnp.concatenate([ref[rows, h * BLK : (h + 1) * BLK] for h in range(heads)], axis=0)


def block_seen(plan_ref, j, local, heads):
    if plan_ref is None:
        key = lax.broadcasted_iota(jnp.int32, (BLK, BLK), 0)
        row = lax.broadcasted_iota(jnp.int32, (BLK, BLK), 1)
        return jnp.concatenate([key <= row] * heads, axis=1)
    me = lax.axis_index("seq")
    odd = lax.rem(plan_ref[0, me * local + j], NB)
    return jnp.full((BLK, heads * BLK), odd, jnp.int32) > 0


def merged(scale, first, second):
    peak = jnp.maximum(first[0], second[0])
    a, b = jnp.exp2((first[0] - peak) * scale), jnp.exp2((second[0] - peak) * scale)
    return peak, first[1] * a + second[1] * b, first[2] * a + second[2] * b


def score_stats(scale, s, dp):
    peak = jnp.max(s, axis=0, keepdims=True)
    e = jnp.exp2(s * scale - peak * scale)
    return peak, jnp.sum(e, axis=0, keepdims=True), jnp.sum(e * dp, axis=0, keepdims=True)


def stats_kernel(scale, shards, own, parts, carried, ordered, *refs):
    refs = list(refs)
    plan_ref = refs.pop(0) if parts else None
    q_ref, w_ref = refs.pop(0), refs.pop(0)
    before = refs.pop(0) if carried else None
    kv = [refs.pop(0) for _ in range(shards)]
    own_ref = refs.pop(0) if own else None
    pieces = [refs.pop(0) for _ in range(parts)]
    refs = refs[ordered:]
    out_ref = refs.pop(0)
    heads, local = q_ref.shape[1] // BLK, q_ref.shape[0] // BLK
    block_stats = None
    if parts:
        own_ref = refs.pop(0)
        join_pieces(pieces, own_ref)
    if own_ref is not None:
        block_stats = []
        for j in range(local):
            pairs = own_ref[j * BLK : (j + 1) * BLK]
            s = dot(pairs[:, KEYS], block_rows(q_ref, j), NT)
            dp = dot(pairs[:, VALUES], block_rows(w_ref, j), NT)
            s = jnp.where(block_seen(plan_ref, j, local, heads), s, BIG_NEGATIVE)
            block_stats.append(score_stats(scale, s, dp))
    for t, r, rows, cols in head_tiles(q_ref):
        q, w = q_ref[rows, cols], w_ref[rows, cols]
        state = None
        if carried:
            state = tuple(before[t, i : i + 1] for i in range(3))
        if block_stats is not None:
            pair = block_stats[2 * r : 2 * r + 2]
            more = tuple(jnp.concatenate([x[i][:, cols] for x in pair], axis=1) for i in range(3))
            state = more if state is None else merged(scale, state, more)
        for ref in kv:
            s, dp = dot(ref[:, KEYS], q, NT), dot(ref[:, VALUES], w, NT)
            if state is None:
                state = score_stats(scale, s, dp)
                continue
            m, l, d = state
            peak = jnp.maximum(m, jnp.max(s, axis=0, keepdims=True))
            shrink = jnp.exp2((m - peak) * scale)
            e = jnp.exp2(s * scale - peak * scale)
            l = l * shrink + jnp.sum(e, axis=0, keepdims=True)
            d = d * shrink + jnp.sum(e * dp, axis=0, keepdims=True)
            state = peak, l, d
        for i in range(3):
            out_ref[t, i : i + 1] = state[i]


def grad_kernel(scale, shards, own, partner, carried, ordered, *refs):
    refs = list(refs)
    plan_ref = refs.pop(0) if partner else None
    q_ref, w_ref, stats_ref = refs.pop(0), refs.pop(0), refs.pop(0)
    before = refs.pop(0) if carried else None
    kv = [refs.pop(0) for _ in range(shards)]
    blocks_ref = refs.pop(0) if own or partner else None
    refs = refs[ordered:]
    dq_ref = refs.pop(0)
    kv_out = refs.pop(0) if shards else None
    kv_sum = refs.pop() if shards else None
    if partner:
        blocks_out, blocks_sum = refs[:partner], refs[partner]
    elif own:
        blocks_sum = refs[0]
    heads, local = q_ref.shape[1] // BLK, q_ref.shape[0] // BLK
    halves = q_ref.shape[0] // TILE
    back = scale / LOG2E

    def factors(rows):
        inverse = 1.0 / rows[1]
        return rows[0] * scale, inverse, rows[2] * inverse

    def grads(s, dp, rows):
        peak, inverse, delta = rows
        p = jnp.exp2(s * scale - peak) * inverse
        return p.astype(BF16), (p * (dp - delta)).astype(BF16)

    def add_queries(dq, rows, cols):
        if carried:
            dq = dq + before[cols, rows]
        dq_ref[cols, rows] = dq

    if blocks_ref is not None:
        for j in range(local):
            place = slice(j * BLK, (j + 1) * BLK)
            lanes = slice((j % 2) * BLK, (j % 2 + 1) * BLK)
            rows = [
                jnp.concatenate(
                    [stats_ref[h * halves + j // 2, i : i + 1, lanes] for h in range(heads)], axis=1
                )
                for i in range(3)
            ]
            q, w = block_rows(q_ref, j), block_rows(w_ref, j)
            keys = blocks_ref[place, KEYS]
            s = jnp.where(block_seen(plan_ref, j, local, heads), dot(keys, q, NT), BIG_NEGATIVE)
            p, ds = grads(s, dot(blocks_ref[place, VALUES], w, NT), factors(rows))
            blocks_sum[place, KEYS] = dot(ds, q, NN) * back
            blocks_sum[place, VALUES] = dot(p, w, NN)
            dq = dot(keys.T, ds, NN)
            for h in range(heads):
                cols = slice(h * BLK, (h + 1) * BLK)
                add_queries(dq[:, cols], place, cols)
        if partner:
            write_pieces(blocks_sum, blocks_out)
    if not shards:
        return
    keys = jnp.concatenate([ref[:, KEYS] for ref in kv], axis=0)
    values = jnp.concatenate([ref[:, VALUES] for ref in kv], axis=0)
    turned = keys.T
    for t, r, rows, cols in head_tiles(q_ref):
        q, w = q_ref[rows, cols], w_ref[rows, cols]
        state = factors([stats_ref[t, i : i + 1] for i in range(3)])
        p, ds = grads(dot(keys, q, NT), dot(values, w, NT), state)
        dk, dv = dot(ds, q, NN), dot(p, w, NN)
        if t == 0:
            kv_sum[:, KEYS] = dk
            kv_sum[:, VALUES] = dv
        else:
            kv_sum[:, KEYS] += dk
            kv_sum[:, VALUES] += dv
        add_queries(dot(turned, ds, NN), rows, cols)
    for side, factor in ((KEYS, back), (VALUES, 1.0)):
        kv_out[:, side] = (kv_sum[:, side] * factor).astype(kv_out.dtype)


def turn_kernel(x_ref, after_ref, out_ref):
    for h in range(x_ref.shape[0] // BLK):
        cols = slice(h * BLK, (h + 1) * BLK)
        out_ref[:, cols] = x_ref[cols, :].T


def finish_kernel(back, start, plan_ref, lengths_ref, *refs):
    total = jnp.int32(0)
    for r in range(RESP):
        total = total + lengths_ref[0, r]
    share = 1.0 / jnp.full((1, BLK), total.astype(F32))
    (dq_ref, own_ref, prompt_ref), pieces = refs[:3], refs[3:-8]
    outs = refs[-8:-5]
    held, dq_out, stream_out, prompt_out, sems = refs[-5:]
    leaving = [dq_out, stream_out, prompt_out]
    copies = [pltpu.make_async_copy(a, b, sems.at[i]) for i, (a, b) in enumerate(zip(leaving, outs))]
    join_pieces(pieces, held, start)
    me = lax.axis_index("seq")
    local = own_ref.shape[0] // BLK
    dq_out[...] = (dq_ref[...] * (share[:, :1] * back)).astype(BF16)
    copies[0].start()
    for cols in (KEYS, VALUES):
        for s in range(local):
            rows = slice(s * BLK, (s + 1) * BLK)
            odd = lax.rem(plan_ref[0, me * local + s], NB)
            odd_rows = jnp.full((BLK, BLK), odd, jnp.int32) > 0
            stream = own_ref[rows, cols] + jnp.where(odd_rows, 0.0, held[rows, cols].astype(F32))
            stream_out[rows, cols] = (stream * share).astype(BF16)
        prompt_out[:, cols] = (prompt_ref[:, cols] * share).astype(BF16)
    for copy in copies[1:]:
        copy.start()
    for copy in copies:
        copy.wait()


def pick_kernel(per, parts, picked, joined, ordered, *refs):
    out_ref, refs = refs[-1], refs[: len(refs) - 1 - ordered]
    if joined:
        piece, refs = refs[-1], refs[:-1]
        first, rows = len(picked) * per, piece.shape[1]
        for s in range(piece.shape[0]):
            out_ref[first + s * rows : first + (s + 1) * rows] = piece[s]
    where = []
    for ref in refs[:parts]:
        where += [(ref, i) for i in range(ref.shape[0] // per)]
    for n, i in enumerate(picked):
        ref, at = where[i]
        total = ref[at * per : (at + 1) * per].astype(F32)
        for other in refs[parts:]:
            total = total + other[i * per : (i + 1) * per].astype(F32)
        out_ref[n * per : (n + 1) * per] = total.astype(out_ref.dtype)


def local(query, resp_kv, prompt_kv, grad_out, rewards, lengths, block_order):
    groups = lax.axis_size("grp")
    count = lax.axis_size("seq")
    q, resp, prompt, grad = query[0], resp_kv[0], prompt_kv[0], grad_out[0]
    rows, width = resp.shape
    blocks = rows // BLK
    heads = q.shape[1] // BLK
    line = count // 2
    scale = LOG2E * BLK**-0.5
    piece = jax.ShapeDtypeStruct((blocks, BLK // line, width), BF16)
    stack = jax.ShapeDtypeStruct((line, *piece.shape), BF16)

    def swap(x, axis, k):
        size = lax.axis_size(axis)
        return lax.ppermute(x, axis, [(i, i ^ k) for i in range(size)])

    def along(sent):
        return [sent[0]] + [swap(sent[k], "seq", 2 * k) for k in range(1, line)]

    def gather_line(name, sent, after=()):
        body = partial(stack_kernel, line)
        return call(body, name, stack, [VMEM] * line, along(sent), after=after)

    def deliver(name, mine, after=()):
        other = swap(mine, "seq", 1)
        return call(
            partial(route_kernel, line),
            name + "_route",
            [piece] * line,
            [SMEM, VMEM, VMEM],
            [block_order, mine, other],
            [pltpu.VMEM((2, *stack.shape), BF16), pltpu.SMEM((block_order.shape[1],), jnp.int32)],
            after=after,
        )

    pieces = call(split_kernel, "pairs_split", [piece] * line, [VMEM], [resp])
    weighted, prompt_on = call(
        partial(weight_kernel, groups),
        "weight_rows",
        [jax.ShapeDtypeStruct(grad.shape, BF16), jax.ShapeDtypeStruct(prompt.shape, BF16)],
        [SMEM, SMEM, SMEM, VMEM, VMEM],
        [block_order, rewards, lengths, grad, prompt],
    )
    mine = gather_line("pairs_stack", pieces, after=[weighted])
    stats_shape = jax.ShapeDtypeStruct((heads * rows // TILE, 8, TILE), F32)

    def stats(name, before, kv, own=None, parts=(), after=(), beside=False):
        args = [block_order] if parts else []
        specs = [SMEM] * len(args)
        args += [q, weighted] + ([before] if before is not None else []) + list(kv)
        args += ([own] if own is not None else []) + list(parts)
        specs += [VMEM] * (len(args) - len(specs))
        out = [stats_shape]
        if parts:
            out.append(jax.ShapeDtypeStruct(resp.shape, BF16))
        body = partial(
            stats_kernel,
            scale,
            len(kv),
            own is not None,
            len(parts),
            before is not None,
            len(after),
        )
        return call(body, name, out, specs, args, after=after, beside=beside)

    (state,) = stats("stats_own", None, [prompt_on], own=resp, after=[mine])
    routed = deliver("pairs", mine, after=[state])
    arrived = along(routed)

    def held_back(x, after):
        same = jax.ShapeDtypeStruct(x.shape, x.dtype)
        return call(pass_kernel, "pass_on", same, [VMEM], [x], after=[after])

    column = {0: prompt_on}
    bit = count // 2
    while bit > 1:
        column.update({k ^ bit: swap(x, "seq", bit) for k, x in column.items()})
        if bit == count // 2 or bit == 2:
            column[bit] = held_back(column[bit], state)
        bit //= 2
    early = [k for k in column if not k & 2 or k == 2]
    late = [k for k in column if k not in early]
    across = {k: swap(column[k] if k else prompt_on, "seq", 1) for k in early}
    coming = [x for k, x in column.items() if k] + [across[k] for k in early]
    (state,) = stats("stats_prompt", state, coming[:2], after=[routed[0]])
    across.update({k: swap(held_back(column[k], state), "seq", 1) for k in late})
    coming = coming[2:]
    while len(coming) > 2:
        (state,) = stats("stats_prompt", state, coming[:2])
        coming = coming[2:]
    state, partner = stats("stats_partner", state, coming, parts=arrived, beside=True)
    (state,) = stats("stats_last", state, [across[k] for k in late])

    def grads(name, before, kv, own=None, part=None, kind=BF16, after=(), beside=False):
        args = [block_order] if part is not None else []
        specs = [SMEM] * len(args)
        args += [q, weighted, state] + ([before] if before is not None else [])
        args += list(kv) + [x for x in (own, part) if x is not None]
        specs += [VMEM] * (len(args) - len(specs))
        keys = sum(x.shape[0] for x in kv)
        out = [jax.ShapeDtypeStruct(q.shape[::-1], F32)]
        out += [jax.ShapeDtypeStruct((keys, width), kind)] if kv else []
        scratch = [pltpu.VMEM((keys, width), F32)] if kv else []
        if own is not None:
            out.append(jax.ShapeDtypeStruct(resp.shape, F32))
        if part is not None:
            out += [piece] * line
            scratch.append(pltpu.VMEM(resp.shape, F32))
        body = partial(
            grad_kernel,
            scale,
            len(kv),
            own is not None,
            line if part is not None else 0,
            before is not None,
            len(after),
        )
        return call(body, name, out, specs, args, scratch, after=after, beside=beside)

    per = prompt.shape[0]

    def pick(name, parts, extra, picked, kind, joined=(), after=(), beside=False):
        args = [*parts, *extra, *joined]
        height = per * len(picked) + sum(x.shape[0] * x.shape[1] for x in joined)
        return call(
            partial(pick_kernel, per, len(parts), tuple(picked), len(joined), len(after)),
            name,
            jax.ShapeDtypeStruct((height, width), kind),
            [VMEM] * len(args),
            args,
            after=after,
            beside=beside,
        )

    near = [k for k in column if k & 2]
    rest = [k for k in column if not k & 2]
    dq, *terms = grads("grads_partner", None, [], part=partner)
    dq, far_near = grads("grads_across", dq, [across[k] for k in near])
    mine = gather_line("terms_stack", terms, after=[far_near])
    far_near = swap(far_near, "seq", 1)
    dq, sums = grads("grads_near", dq, [column[k] for k in near], kind=F32, after=[mine], beside=True)
    dq, far_rest = grads("grads_across", dq, [across[k] for k in rest])
    sums = pick("sum_near", [sums], [far_near], range(len(near)), BF16, after=[far_rest])
    far_rest = swap(far_rest, "seq", 1)
    as_lengths = jax.ShapeDtypeStruct(lengths.shape, jnp.int32)

    def added(x, step, after):
        args = [x, swap(x, "grp", step)]
        return call(add_kernel, "add_lengths", as_lengths, [VMEM] * 2, args, after=[after])

    total = call(pass_kernel, "pass_lengths", as_lengths, [VMEM], [lengths], after=[sums])
    dq, sent = grads("grads_rest", dq, [column[k] for k in rest], kind=F32, after=[sums])
    sums = swap(sums, "seq", 2)
    step = 1
    if step < groups:
        total, step = added(total, step, sent), 2
    routed = deliver("terms", mine, after=[sent])
    returned = {k: routed[k] if k == 0 else swap(routed[k], "seq", 2 * k) for k in range(line) if k != 2}
    dq, own_terms = grads("grads_own", dq, [], own=resp, after=[routed[0]])
    sums_on = call(
        pass_kernel,
        "pass_sums",
        jax.ShapeDtypeStruct(sums.shape, BF16),
        [VMEM],
        [sums],
        after=[own_terms],
        beside=True,
    )
    held, parts, extra, order = rest, [sent], [far_rest, sums_on], []
    bit = 4
    while bit < count:
        keep = [i for i, k in enumerate(held) if not k & bit]
        send = [i for i, k in enumerate(held) if k & bit]
        joined = [routed[2]] if bit == 4 else []
        leaving = pick("sum_far", parts, extra, send, BF16, joined=joined, after=order)
        kept = pick("sum_kept", parts, extra, keep, F32)
        held, parts, extra, order = [held[i] for i in keep], [kept], [swap(leaving, "seq", bit)], []
        if bit == 4:
            returned[2], start = extra[0], per * len(send)
            shape = jax.ShapeDtypeStruct(q.shape, F32)
            turned = call(turn_kernel, "turn_queries", shape, [VMEM], [dq], after=[leaving])
        bit *= 2
    while step < groups:
        total = added(total, step, turned)
        step *= 2
    prompt_sum = pick("sum_prompt", parts, extra, [0], F32, after=[own_terms])
    grad_query, grad_stream, grad_prompt = call(
        partial(finish_kernel, scale / LOG2E, start),
        "over_count",
        [jax.ShapeDtypeStruct(x.shape, BF16) for x in (q, resp, prompt)],
        [SMEM] * 2 + [VMEM] * (3 + line),
        [block_order, total, turned, own_terms, prompt_sum, *[returned[k] for k in range(line)]],
        [
            *[pltpu.VMEM(x.shape, BF16) for x in (resp, q, resp, prompt)],
            pltpu.SemaphoreType.DMA((3,)),
        ],
        out_spec=ANY,
    )
    return grad_query[None], grad_stream[None], grad_prompt[None]


def solution(mesh):
    in_specs = (
        P("grp", "seq", None),
        P("grp", "seq", None),
        P("grp", "seq", None),
        P("grp", "seq", None),
        P("grp", None),
        P("grp", None),
        P("grp", None),
    )
    out_specs = (P("grp", "seq", None), P("grp", "seq", None), P("grp", "seq", None))
    return jax.shard_map(local, mesh=mesh, in_specs=in_specs, out_specs=out_specs, check_vma=False)
```
